512 devices in a mesh: sample: 4 (over x), variant: 16 (over z_lo, y), protein: 8 (over z_hi, core).
Axes of the slice: x: 4, y: 4, z: 16 (z_hi: 4, z_lo: 4; z = z_hi * 4 + z_lo), core: 2. Of those that a mesh axis runs over, the one named last changes fastest.
Arguments:
- dosages: bfloat16 [4096, 16384], P('sample', 'variant'), may hold values from 0 to 2
- proteins: bfloat16 [4096, 2048], P('sample', 'protein'), may hold values from -6 to 6
- covariates: float32 [44, 4096], P(None, 'sample'), may hold values from 0 to 2
- hit_index: int32 [64, 32, 128], P(None, 'protein'), may hold values from 0 to 16383, as said below
- hit_count: int32 [64, 32], P(None, 'protein'), may hold values from 1 to 128, as said below
Outputs:
- zscores: float32 [16384, 2048], P('variant', 'protein')
- hit_gram: float32 [2048, 128, 128], P(('sample', 'variant', 'protein'))
The draws below stay inside these ranges and needn't reach their ends.
Inputs may be any that keep to these rules, and one draw needn't show every extreme that they name: `hit_count`: entry [g, i] is protein g * 32 + i. In every aligned block of 4 proteins the counts sum to exactly 256, and one of them is 128. `hit_index`: entry [g, i, j] is slot j of protein g * 32 + i. For j below the protein's count it is a slab variant, all distinct within one protein; other slots hold 0. Variant block b holds the variants b * 1024 to (b + 1) * 1024 - 1. In every aligned block of 4 proteins exactly 48 live hits lie in one variant block, and the other live hits are spread over the other blocks as evenly as possible.
All inputs are finite; a program needn't handle non-finite values.
Results may differ from the reference program's by a relative error of at most 0.025.
Values may be sent and summed in bfloat16 or wider, within the bound.
A program may use at most 64 MiB of HBM per device.

```python
import jax
import jax.numpy as jnp
from jax import lax

V_DEV = 1024
PROT = 2048
NCOV = 44
HITS = 128
SAMPLES = 4096
VARIANTS = 16384
GROUPS = 64
P_GROUP = 32
P_OWN = 4
TOTAL_HITS = 256
CAP = 48


def hit_tables(key):
    owners = PROT // P_OWN
    blocks = VARIANTS // V_DEV
    owner_keys = jax.random.split(jax.random.fold_in(key, 17), owners)

    def one_owner(owner_key):
        key_full, key_spread, key_label, key_busy, key_offset = jax.random.split(owner_key, 5)
        full_one = jax.random.randint(key_full, (), 0, P_OWN)
        extra_hits = TOTAL_HITS - HITS - (P_OWN - 1)
        spare_slots = (P_OWN - 1) * (HITS - 1)
        shuffled = jax.random.permutation(key_spread, spare_slots)
        chosen = (shuffled < extra_hits).astype(jnp.int32).reshape(P_OWN - 1, HITS - 1).sum(axis=1)
        others = jnp.arange(P_OWN - 1, dtype=jnp.int32)
        target = others + (others >= full_one).astype(jnp.int32)
        counts = jnp.ones((P_OWN,), jnp.int32).at[target].add(chosen).at[full_one].set(HITS)
        live_slot = jnp.arange(HITS, dtype=jnp.int32)[None, :] < counts[:, None]
        flat_live = live_slot.reshape(-1).astype(jnp.int32)
        serial = jnp.clip(jnp.cumsum(flat_live) - 1, 0, TOTAL_HITS - 1)
        shuffle = jax.random.permutation(key_label, TOTAL_HITS)
        labels = shuffle[serial]
        busy_block = jax.random.randint(key_busy, (), 0, blocks)
        other_blk = jnp.mod(labels - CAP, blocks - 1)
        other_blk = other_blk + (other_blk >= busy_block).astype(jnp.int32)
        block_of = jnp.where(labels < CAP, busy_block, other_blk).reshape(P_OWN, HITS)
        slot_ids = jnp.arange(HITS, dtype=jnp.int32)
        earlier = slot_ids[None, :] < slot_ids[:, None]
        matches = (block_of[:, :, None] == block_of[:, None, :]) & live_slot[:, None, :] & earlier[None]
        rank_in = jnp.sum(matches.astype(jnp.int32), axis=2)
        offset_keys = jax.random.split(key_offset, P_OWN)
        offsets = jax.vmap(lambda sub_key: jax.random.permutation(sub_key, V_DEV))(offset_keys).astype(jnp.int32)
        offset_of = jnp.take_along_axis(offsets, rank_in, axis=1)
        variant_of = jnp.where(live_slot, block_of * V_DEV + offset_of, 0).astype(jnp.int32)
        return (variant_of, counts)
    variant_all, count_all = jax.vmap(one_owner)(owner_keys)
    return (variant_all.reshape(PROT, HITS), count_all.reshape(PROT))


def draw_hit_index(key, part):
    return hit_tables(key)[0].reshape(GROUPS, P_GROUP, HITS)


def draw_hit_count(key, part):
    return hit_tables(key)[1].reshape(GROUPS, P_GROUP)


def block_levels(key, shape, shards, low, high):
    def one(axis_at, blocks):
        draws = jax.random.uniform(jax.random.fold_in(jax.random.fold_in(key, 6), axis_at), (blocks,), jnp.float32, low / len(shards), high / len(shards))
        return jnp.repeat(jnp.exp(draws), shape[axis_at] // blocks).reshape((-1,) + (1,) * (len(shape) - axis_at - 1))

    gain = one(*shards[0])
    for cut in shards[1:]:
        gain = gain * one(*cut)
    return gain


def bell_draw(own_key, shape, deviation, limit, shards=(), kind=jnp.bfloat16):
    level = block_levels(own_key, shape, shards, -0.22, 0.18) if shards else 1.0
    entries = jax.random.normal(own_key, shape, jnp.float32) * deviation * level
    return jnp.minimum(jnp.maximum(entries, -limit), limit).astype(kind)


def setup_inputs(seed: int = 0) -> dict:
    key_of = jax.random.split(jax.random.key(seed), 6)
    dosages = jnp.clip(2.0 * jax.random.uniform(key_of[0], (SAMPLES, VARIANTS), jnp.float32) ** block_levels(key_of[0], (SAMPLES, VARIANTS), ((0, 4), (1, 16)), -0.2, 0.2), 0.0, 2.0).astype(jnp.bfloat16)
    proteins = bell_draw(key_of[1], (SAMPLES, PROT), 1.0, 6.0, ((0, 4), (1, 8)))
    covariates = jnp.clip(2.0 * jax.random.uniform(key_of[2], (NCOV, SAMPLES), jnp.float32) ** block_levels(key_of[2], (NCOV, SAMPLES), ((1, 4),), -0.2, 0.2), 0.0, 2.0)
    hit_index = draw_hit_index(jax.random.fold_in(key_of[5], 71), 0)
    hit_count = draw_hit_count(jax.random.fold_in(key_of[5], 71), 0)
    return {"dosages": dosages, "proteins": proteins, "covariates": covariates, "hit_index": hit_index, "hit_count": hit_count}


def reference(dosages, proteins, covariates, hit_index, hit_count):
    largest_value = lax.Precision.HIGHEST
    hit_index = hit_index.reshape(PROT, HITS)
    hit_count = hit_count.reshape(PROT)
    gram_cov = jnp.dot(covariates, covariates.T, precision=largest_value)
    factor = jnp.linalg.cholesky(gram_cov)
    identity = jnp.eye(NCOV, dtype=jnp.float32)
    inverse_factor = jax.scipy.linalg.solve_triangular(factor, identity, lower=True)
    cov_prot = jnp.dot(covariates, proteins.astype(jnp.float32), precision=largest_value)
    coef_mat = jnp.dot(inverse_factor.T, jnp.dot(inverse_factor, cov_prot, precision=largest_value), precision=largest_value)
    residual = (proteins.astype(jnp.float32) - jnp.dot(covariates.T, coef_mat, precision=largest_value)).astype(jnp.bfloat16)
    rss = lax.optimization_barrier(jnp.sum(jnp.square(residual.astype(jnp.float32)), axis=0))
    cov_dos = jnp.dot(covariates, dosages.astype(jnp.float32), precision=largest_value)
    dos_sq = lax.optimization_barrier(jnp.sum(jnp.square(dosages.astype(jnp.float32)), axis=0))
    whiten = jnp.dot(inverse_factor, cov_dos, precision=largest_value)
    dos_var = dos_sq - lax.optimization_barrier(jnp.sum(whiten * whiten, axis=0))
    score = jnp.dot(dosages.T.astype(jnp.float32), residual.astype(jnp.float32), preferred_element_type=jnp.float32)
    freedom = jnp.float32(SAMPLES - NCOV)
    zscores = score / jnp.sqrt(dos_var[:, None] * (rss[None, :] / freedom + 1e-05))

    def one_block(pair):
        index_all, count_all = pair
        width = index_all.shape[0]
        hit_cols = jnp.take(dosages, index_all.reshape(-1), axis=1).reshape(SAMPLES, width, HITS)
        live_slot = jnp.arange(HITS, dtype=jnp.int32)[None, :] < count_all[:, None]
        hit_cols = jnp.where(live_slot[None], hit_cols, jnp.zeros((), jnp.bfloat16))
        hit_expanded = hit_cols.astype(jnp.float32)
        hit_prod = jnp.einsum('spa,spb->pab', hit_expanded, hit_expanded, precision=largest_value)
        hit_covariate_matrix = jnp.einsum('gm,mzh->gzh', covariates, hit_expanded, precision=largest_value)
        decorrelated_scores = jnp.einsum('qz,znf->qnf', inverse_factor, hit_covariate_matrix, precision=largest_value)
        adjustment_term = jnp.einsum('zwr,zwj->wrj', decorrelated_scores, decorrelated_scores, precision=largest_value)
        return (hit_prod - adjustment_term) / jnp.float32(SAMPLES)
    group = 32
    hit_gram = lax.map(one_block, (hit_index.reshape(-1, group, HITS), hit_count.reshape(-1, group)))
    return (zscores, hit_gram.reshape(PROT, HITS, HITS))
```

```python
import jax
import jax.numpy as jnp
from jax import lax
from jax.sharding import PartitionSpec as P

BF16 = jnp.bfloat16
F32 = jnp.float32


def shards(dosages, proteins, covariates, hit_index, hit_count):
    best = lax.Precision.HIGHEST
    n_sample = lax.axis_size("sample")
    n_variant = lax.axis_size("variant")
    rows, v_dev = dosages.shape
    n_prot = proteins.shape[1]
    n_cov = covariates.shape[0]
    samples = rows * n_sample
    n_dest, p_own, slots = hit_index.shape
    flat = p_own * slots
    capacity = 3 * max(p_own * 16, 2 * slots) // n_variant
    my_block = lax.axis_index("variant")

    dos_part = jnp.dot(covariates, dosages, precision=best, preferred_element_type=F32)
    prot_part = jnp.dot(covariates, proteins, precision=best, preferred_element_type=F32)
    gram_part = jnp.dot(covariates, covariates.T, precision=best)
    total = lax.psum(jnp.concatenate([dos_part, prot_part, gram_part], axis=1), "sample")
    gram_cov = total[:, v_dev + n_prot :]
    factor = jnp.linalg.cholesky(gram_cov)
    inverse_factor = jax.scipy.linalg.solve_triangular(
        factor, jnp.eye(n_cov, dtype=F32), lower=True
    )
    coef = jnp.dot(
        inverse_factor.T,
        jnp.dot(inverse_factor, total[:, : v_dev + n_prot], precision=best),
        precision=best,
    )
    fitted = jnp.einsum("cs,cp->sp", covariates, coef, precision=best)
    dos_res = (dosages.astype(F32) - fitted[:, :v_dev]).astype(BF16)
    prot_res = (proteins.astype(F32) - fitted[:, v_dev:]).astype(BF16)

    index_all = hit_index.reshape(n_dest, flat)
    slot_ids = jnp.arange(slots, dtype=jnp.int32)
    live_all = (slot_ids[None, None, :] < hit_count[:, :, None]).reshape(n_dest, flat)
    upper = jnp.triu(jnp.ones((flat, flat), BF16))
    chosen = live_all & (index_all // v_dev == my_block)
    rank = jnp.dot(chosen.astype(BF16), upper, preferred_element_type=F32).astype(jnp.int32) - 1
    rank = jnp.where(chosen, rank, -1)
    local = index_all - my_block * v_dev + 1
    places = jnp.arange(capacity, dtype=jnp.int32)
    col_index = jnp.sum(
        jnp.where(rank[:, None, :] == places[None, :, None], local[:, None, :], 0), axis=2
    )
    pick = (
        col_index.reshape(-1)[:, None] == jnp.arange(1, v_dev + 1, dtype=jnp.int32)[None, :]
    ).astype(BF16)
    outgoing = lax.dot_general(
        pick, dos_res, (((1,), (1,)), ((), ())), preferred_element_type=F32
    ).astype(BF16)
    received = lax.all_to_all(
        outgoing.reshape(n_sample, n_variant, capacity, rows),
        "variant",
        split_axis=1,
        concat_axis=1,
        tiled=True,
    ).reshape(n_sample, n_variant * capacity, rows)

    score = lax.dot_general(
        dos_res, prot_res, (((0,), (0,)), ((), ())), preferred_element_type=F32
    ).astype(BF16)
    squares = jnp.concatenate(
        [
            jnp.sum(jnp.square(dos_res.astype(F32)), axis=0),
            jnp.sum(jnp.square(prot_res.astype(F32)), axis=0),
        ]
    )
    squares = lax.psum(squares, "sample")
    own = v_dev // n_sample
    score = lax.psum_scatter(score, "sample", scatter_dimension=0, tiled=True).astype(F32)
    dos_var = lax.dynamic_slice(squares, (lax.axis_index("sample") * own,), (own,))
    rss = squares[v_dev:]
    z = score / jnp.sqrt(dos_var[:, None] * (rss[None, :] / F32(samples - n_cov) + 1e-05))
    zscores = lax.all_gather(z.astype(BF16), "sample", axis=0, tiled=True).astype(F32)

    own_index = lax.dynamic_slice_in_dim(
        index_all.reshape(n_sample, n_variant, flat), my_block, 1, axis=1
    )[:, 0]
    own_live = lax.dynamic_slice_in_dim(
        live_all.reshape(n_sample, n_variant, flat), my_block, 1, axis=1
    )[:, 0]
    block_of = own_index // v_dev
    member = (
        block_of[:, None, :] == jnp.arange(n_variant, dtype=jnp.int32)[None, :, None]
    ) & own_live[:, None, :]
    upto = jnp.dot(
        member.astype(BF16).reshape(-1, flat), upper, preferred_element_type=F32
    ).reshape(member.shape)
    rank_in = jnp.sum(jnp.where(member, upto, 0.0), axis=1).astype(jnp.int32) - 1
    position = jnp.where(own_live, block_of * capacity + rank_in, -1)
    place = (
        position[:, :, None] == jnp.arange(n_variant * capacity, dtype=jnp.int32)[None, None, :]
    ).astype(BF16)
    cols = (
        jnp.einsum("sjk,skr->sjr", place, received, preferred_element_type=F32)
        .astype(BF16)
        .reshape(n_sample, p_own, slots, rows)
    )
    gram = jnp.einsum("spar,spbr->spab", cols, cols, preferred_element_type=F32)
    gram = lax.psum_scatter(gram.astype(BF16), "sample", scatter_dimension=0, tiled=False)
    return (zscores, gram.astype(F32) / F32(samples))


def solution(mesh):
    in_specs = (
        P("sample", "variant"),
        P("sample", "protein"),
        P(None, "sample"),
        P(None, "protein", None),
        P(None, "protein"),
    )
    out_specs = (P("variant", "protein"), P(("sample", "variant", "protein"), None, None))
    return jax.shard_map(shards, mesh=mesh, in_specs=in_specs, out_specs=out_specs, check_vma=False)
```

```python
import functools

import jax
import jax.numpy as jnp
from jax import lax
from jax.experimental import pallas as pl
from jax.experimental.pallas import tpu as pltpu
from jax.sharding import PartitionSpec as P

BF16 = jnp.bfloat16
F32 = jnp.float32
MESH = pl.DeviceIdType.MESH
BEST = lax.Precision.HIGHEST
NT = (((1,), (1,)), ((), ()))
CHUNKS = 4
CP = 48
CB = 64


def kernel(n_z, n_cov, cap, freedom, dos, prot, cf, c3, ct, col, pos, z_out, g_out, *scratch):
    (
        dall, d2own, d2c, pick, out, rec, fr, fl, arb, bt, bc, prt, ssend, srecv, auxb, auxs, zbuf,
        gacc, gsend, grecv, *sems,
    ) = scratch
    ag, fw, sw, bag, bfw, bsw, ar, sc, ax, zg, gr, yd, yf, yg = zip(sems[0::2], sems[1::2])

    x = lax.axis_index("sample")
    v = lax.axis_index("variant")
    q = lax.axis_index("protein")
    y, zl = lax.rem(v, 4), v // 4
    core, zh = lax.rem(q, 2), q // 2
    z = zh * 4 + zl

    def at_x(d):
        return (lax.rem(x + d, 4), v, q)

    def at_y(d):
        return (x, zl * 4 + lax.rem(y + d, 4), q)

    def at_z(d):
        there = lax.rem(z + d + n_z, n_z)
        return (x, lax.rem(there, 4) * 4 + y, (there // 4) * 2 + core)

    right, left, sibling = at_z(1), at_z(-1), (x, v, zh * 2 + 1 - core)
    up, down = at_y(1), at_y(3)

    neighbours = [at_x(1), at_x(2), at_x(3), up, down, right, left, sibling]
    barrier = pltpu.get_barrier_semaphore()
    for there in neighbours:
        pl.semaphore_signal(barrier, inc=1, device_id=there, device_id_type=MESH)
    pl.semaphore_wait(barrier, len(neighbours))

    sent = []

    def send(src, dst, sem, at, there):
        copy = pltpu.make_async_remote_copy(
            src_ref=src,
            dst_ref=dst,
            send_sem=sem[0].at[at],
            recv_sem=sem[1].at[at],
            device_id=there,
            device_id_type=MESH,
        )
        copy.start()
        sent.append(copy)
        return copy

    rows, v_dev = dos.shape
    n_prot = prot.shape[1]
    crows = rows // CHUNKS
    half = crows // 2
    quarter = half // 2
    wide = v_dev // 2
    mine = pl.multiple_of(core * half, half)
    copies = {}

    def piece(k, more=0, size=half):
        return pl.ds(pl.multiple_of(k * crows + core * half + more, quarter), size)

    def gather_own(k):
        part = dos.at[piece(k)]
        copies["a", k] = send(part, dall.at[0, piece(k)], ag, (k, 0), right)
        copies["b", k] = send(part, dall.at[2, piece(k)], ag, (k, 1), left)

    def gather_on(k):
        high, low = piece(k, quarter, quarter), piece(k, 0, quarter)
        copies["a", k].wait_recv()
        copies["c", k] = send(dall.at[0, high], dall.at[1, high], fw, (k, 0), right)
        copies["s0", k] = send(dall.at[0, piece(k)], dall.at[0, piece(k)], sw, (k, 0), sibling)
        copies["b", k].wait_recv()
        copies["d", k] = send(dall.at[2, low], dall.at[1, low], fw, (k, 1), left)
        copies["s2", k] = send(dall.at[2, piece(k)], dall.at[2, piece(k)], sw, (k, 2), sibling)

    def gather_far(k):
        copies["c", k].wait_recv()
        copies["d", k].wait_recv()
        copies["s1", k] = send(dall.at[1, piece(k)], dall.at[1, piece(k)], sw, (k, 1), sibling)

    gather_own(0)
    gather_own(1)

    ours = pl.multiple_of(core * wide, wide)
    c3v = c3[...]
    cd = jnp.dot(c3v, dos[:, pl.ds(ours, wide)], preferred_element_type=F32)
    cq = jnp.dot(c3v, prot[...], preferred_element_type=F32)
    cc = lax.dot_general(cf[...], cf[...], NT, precision=BEST, preferred_element_type=F32)
    arb[x, :, 0:wide] = cd[0:CP] + cd[CP : 2 * CP] + cd[2 * CP :]
    arb[x, :, wide : wide + n_prot] = cq[0:CP] + cq[CP : 2 * CP] + cq[2 * CP :]
    arb[x, :, wide + n_prot :] = jnp.zeros((CP, 128), F32)
    arb[x, :, wide + n_prot : wide + n_prot + CP] = cc
    sums = [send(arb.at[x], arb.at[x], ar, d - 1, at_x(d)) for d in (1, 2, 3)]

    tile = 512
    per_row = 4 * v_dev // tile

    def build(step, carry):
        row, part = step // per_row, lax.rem(step, per_row)
        places = lax.broadcasted_iota(jnp.int32, (4 * cap, tile), 1) + (part * tile + 1)
        hit = jnp.where(col[row] == places, 1.0, 0.0).astype(BF16)
        pick[row, :, pl.ds(pl.multiple_of(part * tile, tile), tile)] = hit
        return carry

    lax.fori_loop(0, 4 * per_row, build, 0)

    gather_on(0)
    gather_own(2)

    for copy in sums:
        copy.wait_recv()
    total = arb[0] + arb[1] + arb[2] + arb[3]
    lane = lax.broadcasted_iota(jnp.int32, (CP, 128), 1)
    row = lax.broadcasted_iota(jnp.int32, (CP, 128), 0)
    both = total[:, wide + n_prot :]
    both = both + jnp.where((lane == row) & (row >= n_cov), 1.0, 0.0)
    both = both + jnp.where(lane == row + 64, 1.0, 0.0)
    unit = lax.broadcasted_iota(jnp.int32, (CP, 1), 0)
    for i in range(n_cov):
        scaled = both[i : i + 1, :] / both[i : i + 1, i : i + 1]
        both = both - (both[:, i : i + 1] - jnp.where(unit == i, 1.0, 0.0)) * scaled
    inverse = pltpu.roll(both, 64, 1)[:, 0:CP]
    coef = jnp.dot(
        inverse, total[:, : wide + n_prot], precision=BEST, preferred_element_type=F32
    )

    bt[0, core, 0:CP, :] = coef[:, :wide].astype(BF16)
    bt[0, core, CP:CB, :] = jnp.zeros((CB - CP, wide), BF16)
    low, high = pl.ds(0, CB // 2), pl.ds(CB // 2, CB // 2)
    b_a = send(bt.at[0, core], bt.at[1, core], bag, 0, right)
    b_b = send(bt.at[0, core], bt.at[3, core], bag, 1, left)
    b_s = [send(bt.at[0, core], bt.at[0, core], bsw, 0, sibling)]

    gather_on(1)
    gather_own(3)
    gather_far(0)

    cb = coef[:, wide:]
    ch = cb.astype(BF16)
    cm = (cb - ch.astype(F32)).astype(BF16)
    gap = jnp.zeros((CB - CP, n_prot), BF16)
    ctv = ct[...]
    fit = jnp.dot(ctv, jnp.concatenate([ch, gap, ch, gap]), preferred_element_type=F32)
    fit = fit + jnp.dot(ctv, jnp.concatenate([cm, gap, cm, gap]), preferred_element_type=F32)
    res = (prot[...].astype(F32) - fit).astype(BF16).astype(F32)
    auxb[x, :, v_dev:] = jnp.broadcast_to(
        jnp.sum(res * res, axis=0, keepdims=True), (8, n_prot)
    )
    prt[...] = res.T.astype(BF16)

    b_a.wait_recv()
    b_c = send(bt.at[1, core, high], bt.at[2, core, high], bfw, 0, right)
    b_s.append(send(bt.at[1, core], bt.at[1, core], bsw, 1, sibling))
    b_b.wait_recv()
    b_d = send(bt.at[3, core, low], bt.at[2, core, low], bfw, 1, left)
    b_s.append(send(bt.at[3, core], bt.at[3, core], bsw, 2, sibling))

    def stack(slot):
        for side in range(2):
            part = bt[slot, side]
            bc[slot, 0:CB, side * wide : (side + 1) * wide] = part
            bc[slot, CB:, side * wide : (side + 1) * wide] = part

    b_s[0].wait_recv()
    stack(0)

    def own_residual(k, squares):
        here = pl.ds(pl.multiple_of(k * crows, crows), crows)
        fit = jnp.dot(ct[here, :], bc[0], preferred_element_type=F32)
        res = dos[here, :].astype(F32) - fit
        d2own[here, :] = res.astype(BF16)
        return squares + jnp.sum(res * res, axis=0, keepdims=True)

    squares = lax.fori_loop(0, CHUNKS, own_residual, jnp.zeros((1, v_dev), F32))
    auxb[x, :, :v_dev] = jnp.broadcast_to(squares, (8, v_dev))
    own = v_dev // 4

    def score(i, carry):
        cols = pl.ds(pl.multiple_of(i * own, own), own)
        ssend[i] = jnp.dot(prt[...], d2own[:, cols], preferred_element_type=F32).astype(BF16)
        return carry

    lax.fori_loop(0, 4, score, 0)
    s_c = [
        send(ssend.at[lax.rem(x + d, 4)], srecv.at[d - 1], sc, d - 1, at_x(d)) for d in (1, 2, 3)
    ]
    a_c = [send(auxb.at[x], auxb.at[x], ax, d - 1, at_x(d)) for d in (1, 2, 3)]

    gather_on(2)
    gather_far(1)
    b_c.wait_recv()
    b_d.wait_recv()
    b_s.append(send(bt.at[2, core], bt.at[2, core], bsw, 3, sibling))
    for copy in b_s[1:]:
        copy.wait_recv()
    for slot in (1, 2, 3):
        stack(slot)

    def choose(k):
        here = pl.ds(k * crows, crows)
        for slot in range(3):
            copies["s%d" % slot, k].wait_recv()
            fit = jnp.dot(ct[here, :], bc[slot + 1], preferred_element_type=F32)
            d2c[slot] = (dall[slot, here, :].astype(F32) - fit).astype(BF16)

        def one(to, carry):
            part = lax.dot_general(
                pick[to, :, 0:v_dev], d2own[here, :], NT, preferred_element_type=F32
            )
            for slot in range(3):
                part = part + lax.dot_general(
                    pick[to, :, (slot + 1) * v_dev : (slot + 2) * v_dev],
                    d2c[slot],
                    NT,
                    preferred_element_type=F32,
                )
            out[k, to] = part.astype(BF16)
            return carry

        lax.fori_loop(0, 4, one, 0)
        ahead, behind, across = lax.rem(y + 1, 4), lax.rem(y + 3, 4), lax.rem(y + 2, 4)
        first, second = pl.ds(0, 2 * cap), pl.ds(2 * cap, 2 * cap)
        copies["f0", k] = send(out.at[k, across, first], fr.at[k], yf, (k, 0), up)
        copies["f1", k] = send(out.at[k, across, second], fl.at[k], yf, (k, 1), down)
        copies["y0", k] = send(out.at[k, ahead], rec.at[k, y], yd, (k, 0), up)
        copies["y1", k] = send(out.at[k, behind], rec.at[k, y], yd, (k, 1), down)
        rec[k, y] = out[k, y]

    def pass_on(k):
        ahead, behind = lax.rem(y + 1, 4), lax.rem(y + 3, 4)
        first, second = pl.ds(0, 2 * cap), pl.ds(2 * cap, 2 * cap)
        copies["f0", k].wait_recv()
        copies["g0", k] = send(fr.at[k], rec.at[k, behind, first], yg, (k, 0), up)
        copies["f1", k].wait_recv()
        copies["g1", k] = send(fl.at[k], rec.at[k, ahead, second], yg, (k, 1), down)

    def gram(k):
        for name in ("y0", "y1", "g0", "g1"):
            copies[name, k].wait_recv()

        def one(to, carry):
            lines = pl.ds(pl.multiple_of(to * cap, cap), cap)
            got = jnp.concatenate([rec[k, i, lines, :] for i in range(4)])
            places = lax.broadcasted_iota(jnp.int32, (4 * 128, 4 * cap), 1)
            place = jnp.where(pos[to] == places, 1.0, 0.0).astype(BF16)
            hits = jnp.dot(place, got, preferred_element_type=F32).astype(BF16)
            for p in range(4):
                h = hits[p * 128 : (p + 1) * 128]
                g = lax.dot_general(h, h, NT, preferred_element_type=F32)
                if k == 0:
                    gacc[to, p] = g
                else:
                    gacc[to, p] = gacc[to, p] + g
            return carry

        lax.fori_loop(0, 4, one, 0)

    choose(0)

    for copy in s_c + a_c:
        copy.wait_recv()
    auxs[...] = auxb[0] + auxb[1] + auxb[2] + auxb[3]
    quarter_v = pl.ds(pl.multiple_of(x * own, own), own)
    dos_var = auxs[0:1, quarter_v]
    rss = auxs[0:1, v_dev:]
    whole = ssend[x].astype(F32)
    for d in range(3):
        whole = whole + srecv[d].astype(F32)
    whole = (whole / jnp.sqrt(dos_var)).T / jnp.sqrt(rss / freedom + 1e-05)
    zbuf[quarter_v, :] = whole.astype(BF16)
    z_c = [send(zbuf.at[quarter_v], zbuf.at[quarter_v], zg, d - 1, at_x(d)) for d in (1, 2, 3)]

    gather_on(3)
    gather_far(2)
    choose(1)
    pass_on(0)
    gather_far(3)
    choose(2)
    pass_on(1)
    gram(0)
    choose(3)
    pass_on(2)
    gram(1)
    pass_on(3)
    gram(2)
    for copy in z_c:
        copy.wait_recv()
    z_out[...] = zbuf[...]
    gram(3)
    gsend[...] = gacc[...].astype(BF16)
    g_c = [
        send(gsend.at[lax.rem(x + d, 4)], grecv.at[d - 1], gr, d - 1, at_x(d)) for d in (1, 2, 3)
    ]
    whole = gacc[x]
    for d in range(3):
        g_c[d].wait_recv()
        whole = whole + grecv[d].astype(F32)
    g_out[...] = whole
    for copy in sent:
        copy.wait_send()


def shards(n_z, dosages, proteins, covariates, hit_index, hit_count):
    n_sample = lax.axis_size("sample")
    n_variant = lax.axis_size("variant")
    rows, v_dev = dosages.shape
    n_prot = proteins.shape[1]
    n_cov = covariates.shape[0]
    samples = rows * n_sample
    n_dest, p_own, slots = hit_index.shape
    flat = p_own * slots
    block_hits = max(p_own * 16, 2 * slots)
    most = 3 * block_hits // n_variant
    other = -(-(block_hits - most) // (n_variant - 1))
    cap = -(-(most + 3 * other) // 16) * 16
    v = lax.axis_index("variant")
    y, zl = lax.rem(v, 4), v // 4

    lists = hit_index.reshape(n_sample, 4, 4, flat)
    lists = lax.dynamic_index_in_dim(lists, zl, 1, keepdims=False).transpose(1, 0, 2)
    slot_ids = jnp.arange(slots, dtype=jnp.int32)
    live = slot_ids < lax.dynamic_index_in_dim(
        hit_count.reshape(n_sample, 4, 4, p_own), zl, 1, keepdims=False
    ).transpose(1, 0, 2)[..., None]
    live = live.reshape(4, n_sample, flat)
    block = lists // v_dev
    upper = jnp.triu(jnp.ones((flat, flat), BF16))

    chosen = live & (block % 4 == y)
    rank = jnp.dot(chosen.astype(BF16), upper, preferred_element_type=F32).astype(jnp.int32) - 1
    rank = jnp.where(chosen, rank, -1)
    column = lists - block * v_dev + ((zl - block // 4) % 4) * v_dev + 1
    places = jnp.arange(cap, dtype=jnp.int32)
    col = jnp.sum(
        jnp.where(rank[:, :, None, :] == places[:, None], column[:, :, None, :], 0), axis=3
    ).reshape(4, n_sample * cap, 1)

    own_live = lax.dynamic_index_in_dim(live, y, 0, keepdims=False)
    own_line = lax.dynamic_index_in_dim(block, y, 0, keepdims=False) % 4
    member = own_live[:, None, :] & (own_line[:, None, :] == jnp.arange(4)[:, None])
    upto = jnp.dot(member.astype(BF16), upper, preferred_element_type=F32)
    rank_in = jnp.sum(jnp.where(member, upto, 0.0), axis=1).astype(jnp.int32) - 1
    pos = jnp.where(own_live, own_line * cap + rank_in, -1).reshape(n_sample, flat, 1)

    cf = jnp.pad(covariates, ((0, CP - n_cov), (0, 0)))
    part = lax.reduce_precision(cf, 8, 7)
    rest = cf - part
    middle = lax.reduce_precision(rest, 8, 7)
    last = rest - middle
    c3 = jnp.concatenate([part, middle, last]).astype(BF16)
    gap = jnp.zeros((CB - CP, rows), F32)
    ct = jnp.concatenate([part, gap, middle, gap]).T.astype(BF16)

    def vmem(shape, dtype=BF16):
        return pltpu.VMEM(shape, dtype)

    def pair(shape):
        return [pltpu.SemaphoreType.DMA(shape)] * 2

    crows = rows // CHUNKS
    own = v_dev // 4
    scratch = [
        vmem((3, rows, v_dev)),
        vmem((rows, v_dev)),
        vmem((3, crows, v_dev)),
        vmem((4, 4 * cap, 4 * v_dev)),
        vmem((CHUNKS, 4, 4 * cap, crows)),
        vmem((CHUNKS, 4, 4 * cap, crows)),
        vmem((CHUNKS, 2 * cap, crows)),
        vmem((CHUNKS, 2 * cap, crows)),
        vmem((4, CP, v_dev // 2 + n_prot + 128), F32),
        vmem((4, 2, CB, v_dev // 2)),
        vmem((4, 2 * CB, v_dev)),
        vmem((n_prot, rows)),
        vmem((4, n_prot, own)),
        vmem((3, n_prot, own)),
        vmem((4, 8, v_dev + n_prot), F32),
        vmem((8, v_dev + n_prot), F32),
        vmem((v_dev, n_prot)),
        vmem((4, p_own, slots, slots), F32),
        vmem((4, p_own, slots, slots)),
        vmem((3, p_own, slots, slots)),
        *pair((CHUNKS, 2)),
        *pair((CHUNKS, 2)),
        *pair((CHUNKS, 3)),
        *pair((2,)),
        *pair((2,)),
        *pair((4,)),
        *pair((3,)),
        *pair((3,)),
        *pair((3,)),
        *pair((3,)),
        *pair((3,)),
        *pair((CHUNKS, 2)),
        *pair((CHUNKS, 2)),
        *pair((CHUNKS, 2)),
    ]
    z, g = pl.pallas_call(
        functools.partial(kernel, n_z, n_cov, cap, float(samples - n_cov)),
        out_shape=(
            jax.ShapeDtypeStruct((v_dev, n_prot), BF16),
            jax.ShapeDtypeStruct((p_own, slots, slots), F32),
        ),
        in_specs=[pl.BlockSpec(memory_space=pltpu.VMEM)] * 7,
        out_specs=(pl.BlockSpec(memory_space=pltpu.VMEM),) * 2,
        scratch_shapes=scratch,
        compiler_params=pltpu.CompilerParams(
            collective_id=0, has_side_effects=True, vmem_limit_bytes=58 * 1024 * 1024
        ),
    )(dosages, proteins, cf, c3, ct, col, pos)
    return (z.astype(F32), g / F32(samples))


def solution(mesh):
    in_specs = (
        P("sample", "variant"),
        P("sample", "protein"),
        P(None, "sample"),
        P(None, "protein", None),
        P(None, "protein"),
    )
    out_specs = (P("variant", "protein"), P(("sample", "variant", "protein"), None, None))
    n_z = 4 * (mesh.shape["protein"] // 2)
    return jax.shard_map(
        functools.partial(shards, n_z),
        mesh=mesh,
        in_specs=in_specs,
        out_specs=out_specs,
        check_vma=False,
    )
```

```python
import functools

import jax
import jax.numpy as jnp
from jax import lax
from jax.experimental import pallas as pl
from jax.experimental.pallas import tpu as pltpu
from jax.sharding import PartitionSpec as P

BF16 = jnp.bfloat16
F32 = jnp.float32
MESH = pl.DeviceIdType.MESH
BEST = lax.Precision.HIGHEST
NT = (((1,), (1,)), ((), ()))
CHUNKS = 4
CP = 48
CB = 64


def kernel(n_z, n_cov, cap, freedom, dos, prot, cov, hidx, hcnt, z_out, g_out, *scratch):
    (
        dall, d2own, pick, out, rec, fr, fl, arb, bt, bc, prt, ssend, srecv, auxb, auxs, zbuf,
        gacc, gsend, grecv, cf, ct, c2, ranks, places, slot_pos, lows, highs, place,
        bout, brec, bfr, bfl, bsel, *sems,
    ) = scratch
    ag, fw, sw, bag, bfw, bsw, ar, sc, ax, zg, gr, yd, yf, yg, hd, hf, hg = zip(sems[0::2], sems[1::2])

    x = lax.axis_index("sample")
    v = lax.axis_index("variant")
    q = lax.axis_index("protein")
    y, zl = lax.rem(v, 4), v // 4
    core, zh = lax.rem(q, 2), q // 2
    z = zh * 4 + zl

    def at_x(d):
        return (lax.rem(x + d, 4), v, q)

    def at_y(d):
        return (x, zl * 4 + lax.rem(y + d, 4), q)

    def at_z(d):
        there = lax.rem(z + d + n_z, n_z)
        return (x, lax.rem(there, 4) * 4 + y, (there // 4) * 2 + core)

    right, left, sibling = at_z(1), at_z(-1), (x, v, zh * 2 + 1 - core)
    up, down = at_y(1), at_y(3)

    neighbours = [at_x(1), at_x(2), at_x(3), up, down, right, left, sibling]
    barrier = pltpu.get_barrier_semaphore()
    for there in neighbours:
        pl.semaphore_signal(barrier, inc=1, device_id=there, device_id_type=MESH)
    pl.semaphore_wait(barrier, len(neighbours))

    sent = []

    def send(src, dst, sem, at, there):
        copy = pltpu.make_async_remote_copy(
            src_ref=src,
            dst_ref=dst,
            send_sem=sem[0].at[at],
            recv_sem=sem[1].at[at],
            device_id=there,
            device_id_type=MESH,
        )
        copy.start()
        sent.append(copy)
        return copy

    rows, v_dev = dos.shape
    n_prot = prot.shape[1]
    slots = hidx.shape[2]
    crows = rows // CHUNKS
    half = crows // 2
    quarter = half // 2
    wide = v_dev // 2
    mine = pl.multiple_of(core * half, half)
    copies = {}

    def piece(k, more=0, size=half):
        return pl.ds(pl.multiple_of(k * crows + core * half + more, quarter), size)

    def gather_own(k):
        part = dos.at[piece(k)]
        copies["a", k] = send(part, dall.at[0, piece(k)], ag, (k, 0), right)
        copies["b", k] = send(part, dall.at[2, piece(k)], ag, (k, 1), left)

    def gather_on(k):
        high, low = piece(k, quarter, quarter), piece(k, 0, quarter)
        copies["a", k].wait_recv()
        copies["c", k] = send(dall.at[0, high], dall.at[1, high], fw, (k, 0), right)
        copies["s0", k] = send(dall.at[0, piece(k)], dall.at[0, piece(k)], sw, (k, 0), sibling)
        copies["b", k].wait_recv()
        copies["d", k] = send(dall.at[2, low], dall.at[1, low], fw, (k, 1), left)
        copies["s2", k] = send(dall.at[2, piece(k)], dall.at[2, piece(k)], sw, (k, 2), sibling)

    def gather_far(k):
        copies["c", k].wait_recv()
        copies["d", k].wait_recv()
        copies["s1", k] = send(dall.at[1, piece(k)], dall.at[1, piece(k)], sw, (k, 1), sibling)

    def choose(k):
        here = pl.ds(k * crows, crows)
        for slot in range(3):
            copies["s%d" % slot, k].wait_recv()

        def one(to, carry):
            part = lax.dot_general(
                pick[to, :, 0:v_dev], dos[here, :], NT, preferred_element_type=F32
            )
            for slot in range(3):
                part = part + lax.dot_general(
                    pick[to, :, (slot + 1) * v_dev : (slot + 2) * v_dev],
                    dall[slot, here, :],
                    NT,
                    preferred_element_type=F32,
                )
            out[k, to] = part.astype(BF16)
            return carry

        lax.fori_loop(0, 4, one, 0)
        ahead, behind, across = lax.rem(y + 1, 4), lax.rem(y + 3, 4), lax.rem(y + 2, 4)
        first, second = pl.ds(0, 2 * cap), pl.ds(2 * cap, 2 * cap)
        copies["f0", k] = send(out.at[k, across, first], fr.at[k], yf, (k, 0), up)
        copies["f1", k] = send(out.at[k, across, second], fl.at[k], yf, (k, 1), down)
        copies["y0", k] = send(out.at[k, ahead], rec.at[k, y], yd, (k, 0), up)
        copies["y1", k] = send(out.at[k, behind], rec.at[k, y], yd, (k, 1), down)
        rec[k, y] = out[k, y]

    def pass_on(k):
        ahead, behind = lax.rem(y + 1, 4), lax.rem(y + 3, 4)
        first, second = pl.ds(0, 2 * cap), pl.ds(2 * cap, 2 * cap)
        copies["f0", k].wait_recv()
        copies["g0", k] = send(fr.at[k], rec.at[k, behind, first], yg, (k, 0), up)
        copies["f1", k].wait_recv()
        copies["g1", k] = send(fl.at[k], rec.at[k, ahead, second], yg, (k, 1), down)

    def gram(k):
        for name in ("y0", "y1", "g0", "g1"):
            copies[name, k].wait_recv()

        done = []
        for d in (2, 1, 3, 0):
            to = lax.rem(x + d, 4)
            lines = pl.ds(pl.multiple_of(to * cap, cap), cap)
            got = jnp.concatenate([rec[k, i, lines, :] for i in range(4)])
            fit = jnp.dot(
                bsel[to], c2[:, k * crows : (k + 1) * crows], preferred_element_type=F32
            )
            got = (got.astype(F32) - fit).astype(BF16)
            hits = jnp.dot(place[to], got, preferred_element_type=F32).astype(BF16)
            for p in range(4):
                h = hits[p * 128 : (p + 1) * 128]
                g = lax.dot_general(h, h, NT, preferred_element_type=F32)
                if k > 0:
                    g = gacc[to, p] + g
                if k == CHUNKS - 1 and d > 0:
                    gsend[d - 1, p] = g.astype(BF16)
                else:
                    gacc[to, p] = g
            if k == CHUNKS - 1 and d > 0:
                done.append(send(gsend.at[d - 1], grecv.at[d - 1], gr, d - 1, at_x(d)))
        return done

    gather_own(0)
    gather_own(1)

    ours = pl.multiple_of(core * wide, wide)
    cf[0:n_cov, :] = cov[...]
    cf[n_cov:, :] = jnp.zeros((CP - n_cov, rows), F32)
    cv = cf[...]
    c_1 = cv.astype(BF16)
    c_2 = (cv - c_1.astype(F32)).astype(BF16)
    c_3 = (cv - c_1.astype(F32) - c_2.astype(F32)).astype(BF16)
    c3v = jnp.concatenate([c_1, c_2, c_3])
    gap = jnp.zeros((CB - CP, rows), F32)
    stacked = jnp.concatenate([c_1.astype(F32), gap, c_2.astype(F32), gap])
    c2[...] = stacked.astype(BF16)
    ct[...] = stacked.T.astype(BF16)
    cd = jnp.dot(c3v, dos[:, pl.ds(ours, wide)], preferred_element_type=F32)
    cq = jnp.dot(c3v, prot[...], preferred_element_type=F32)
    cc = lax.dot_general(cv, cv, NT, precision=BEST, preferred_element_type=F32)
    arb[x, :, 0:wide] = cd[0:CP] + cd[CP : 2 * CP] + cd[2 * CP :]
    arb[x, :, wide : wide + n_prot] = cq[0:CP] + cq[CP : 2 * CP] + cq[2 * CP :]
    arb[x, :, wide + n_prot :] = jnp.zeros((CP, 128), F32)
    arb[x, :, wide + n_prot : wide + n_prot + CP] = cc
    sums = [send(arb.at[x], arb.at[x], ar, d - 1, at_x(d)) for d in (1, 2, 3)]

    flat = 4 * slots
    lane = lax.broadcasted_iota(jnp.int32, (1, slots), 1)
    lists, lives = [], []
    for yy in range(4):
        for s in range(4):
            g = s * 16 + zl * 4 + yy
            lists.append(jnp.concatenate([hidx[g, p : p + 1, :] for p in range(4)], axis=1))
            lives.append(
                jnp.concatenate([lane < hcnt[g, p : p + 1, :] for p in range(4)], axis=1)
            )
    lists = jnp.concatenate(lists).astype(F32)
    lives = jnp.concatenate([jnp.where(one, 1.0, 0.0) for one in lives])
    block = jnp.floor(lists * (1.0 / v_dev))
    far = jnp.floor(block * 0.25)
    line = block - 4.0 * far
    upper = jnp.where(
        lax.broadcasted_iota(jnp.int32, (flat, flat), 0)
        <= lax.broadcasted_iota(jnp.int32, (flat, flat), 1),
        1.0,
        0.0,
    ).astype(BF16)
    chosen = jnp.where(line == y.astype(F32), lives, 0.0)
    rank = jnp.dot(chosen.astype(BF16), upper, preferred_element_type=F32)
    ranks[...] = jnp.where(chosen > 0.0, rank, 0.0)
    slot = zl.astype(F32) - far
    slot = jnp.where(slot < 0.0, slot + 4.0, slot)
    places[...] = lists + (slot - block) * v_dev + 1.0
    pos_of = jnp.where(lives > 0.0, line * cap, -1.0)
    for i in range(4):
        member = jnp.where(line == i, lives, 0.0)
        rank = jnp.dot(member.astype(BF16), upper, preferred_element_type=F32)
        pos_of = pos_of + jnp.where(member > 0.0, rank - 1.0, 0.0)
    slot_pos[...] = pos_of

    def column(t, carry):
        order = lax.broadcasted_iota(jnp.int32, (cap, flat), 0).astype(F32) + 1.0
        found = jnp.where(ranks[pl.ds(t, 1), :] == order, places[pl.ds(t, 1), :], 0.0)
        found = jnp.sum(found, axis=1, keepdims=True) - 1.0
        high = jnp.floor(found * (1.0 / 256.0))
        lows[t] = jnp.broadcast_to(found - 256.0 * high, (cap, 128)).astype(BF16)
        highs[t] = jnp.broadcast_to(high, (cap, 128)).astype(BF16)
        return carry

    lax.fori_loop(0, 16, column, 0)

    near = lax.broadcasted_iota(jnp.int32, (cap, 128), 1).astype(F32)
    near = (near.astype(BF16), (near + 128.0).astype(BF16))
    one_b, zero_b = jnp.ones((cap, 128), BF16), jnp.zeros((cap, 128), BF16)

    def build(t, carry):
        lines = pl.ds(pl.multiple_of(lax.rem(t, 4) * cap, cap), cap)
        low_of, high_of = lows[t], highs[t]
        for part in range(4 * v_dev // 256):
            here = jnp.where(high_of == jnp.full((cap, 128), part, BF16), low_of, -one_b)
            for i in range(2):
                at = part * 256 + i * 128
                pick[t // 4, lines, at : at + 128] = jnp.where(here == near[i], one_b, zero_b)
        return carry

    lax.fori_loop(0, 8, build, 0)
    gather_on(0)
    gather_own(2)
    lax.fori_loop(8, 16, build, 0)
    gather_on(1)
    gather_own(3)
    gather_far(0)
    choose(0)

    def put(s, carry):
        want = jnp.broadcast_to(slot_pos[pl.ds(y * 4 + s, 1), :], (128, flat)).T
        here = lax.broadcasted_iota(jnp.int32, (flat, 128), 1).astype(F32)
        for i in range(4 * cap // 128):
            place[s, :, i * 128 : (i + 1) * 128] = jnp.where(
                want == here + float(i * 128), 1.0, 0.0
            ).astype(BF16)
        return carry

    lax.fori_loop(0, 4, put, 0)

    gather_far(1)
    choose(1)

    for copy in sums:
        copy.wait_recv()
    total = arb[0] + arb[1] + arb[2] + arb[3]
    lane = lax.broadcasted_iota(jnp.int32, (CP, 128), 1)
    row = lax.broadcasted_iota(jnp.int32, (CP, 128), 0)
    both = total[:, wide + n_prot :]
    both = both + jnp.where((lane == row) & (row >= n_cov), 1.0, 0.0)
    both = both + jnp.where(lane == row + 64, 1.0, 0.0)
    unit = lax.broadcasted_iota(jnp.int32, (CP, 1), 0)
    for i in range(n_cov):
        scaled = both[i : i + 1, :] / both[i : i + 1, i : i + 1]
        both = both - (both[:, i : i + 1] - jnp.where(unit == i, 1.0, 0.0)) * scaled
    inverse = pltpu.roll(both, 64, 1)[:, 0:CP]
    coef = jnp.dot(
        inverse, total[:, : wide + n_prot], precision=BEST, preferred_element_type=F32
    )

    bt[0, core, 0:CP, :] = coef[:, :wide].astype(BF16)
    bt[0, core, CP:CB, :] = jnp.zeros((CB - CP, wide), BF16)
    low, high = pl.ds(0, CB // 2), pl.ds(CB // 2, CB // 2)
    b_a = send(bt.at[0, core], bt.at[1, core], bag, 0, right)
    b_b = send(bt.at[0, core], bt.at[3, core], bag, 1, left)
    b_s = [send(bt.at[0, core], bt.at[0, core], bsw, 0, sibling)]

    gather_on(2)
    pass_on(0)
    gather_far(2)
    choose(2)
    gather_on(3)
    pass_on(1)

    cb = coef[:, wide:]
    ch = cb.astype(BF16)
    cm = (cb - ch.astype(F32)).astype(BF16)
    gap = jnp.zeros((CB - CP, n_prot), BF16)
    ctv = ct[...]
    fit = jnp.dot(ctv, jnp.concatenate([ch, gap, ch, gap]), preferred_element_type=F32)
    fit = fit + jnp.dot(ctv, jnp.concatenate([cm, gap, cm, gap]), preferred_element_type=F32)
    res = (prot[...].astype(F32) - fit).astype(BF16).astype(F32)
    auxb[x, :, v_dev:] = jnp.broadcast_to(
        jnp.sum(res * res, axis=0, keepdims=True), (8, n_prot)
    )
    prt[...] = res.T.astype(BF16)

    b_a.wait_recv()
    b_c = send(bt.at[1, core, high], bt.at[2, core, high], bfw, 0, right)
    b_s.append(send(bt.at[1, core], bt.at[1, core], bsw, 1, sibling))
    b_b.wait_recv()
    b_d = send(bt.at[3, core, low], bt.at[2, core, low], bfw, 1, left)
    b_s.append(send(bt.at[3, core], bt.at[3, core], bsw, 2, sibling))

    b_s[0].wait_recv()
    for side in range(2):
        part = bt[0, side]
        bc[0:CB, side * wide : (side + 1) * wide] = part
        bc[CB:, side * wide : (side + 1) * wide] = part


    def own_residual(k, squares):
        here = pl.ds(pl.multiple_of(k * crows, crows), crows)
        fit = jnp.dot(ct[here, :], bc[...], preferred_element_type=F32)
        res = dos[here, :].astype(F32) - fit
        d2own[here, :] = res.astype(BF16)
        return squares + jnp.sum(res * res, axis=0, keepdims=True)

    squares = lax.fori_loop(0, CHUNKS, own_residual, jnp.zeros((1, v_dev), F32))
    auxb[x, :, :v_dev] = jnp.broadcast_to(squares, (8, v_dev))
    own = v_dev // 4

    def score(i, carry):
        cols = pl.ds(pl.multiple_of(i * own, own), own)
        ssend[i] = jnp.dot(prt[...], d2own[:, cols], preferred_element_type=F32).astype(BF16)
        return carry

    lax.fori_loop(0, 4, score, 0)
    s_c = [
        send(ssend.at[lax.rem(x + d, 4)], srecv.at[d - 1], sc, d - 1, at_x(d)) for d in (1, 2, 3)
    ]
    a_c = [send(auxb.at[x], auxb.at[x], ax, d - 1, at_x(d)) for d in (1, 2, 3)]

    gather_far(3)
    choose(3)
    pass_on(2)

    b_c.wait_recv()
    b_d.wait_recv()
    b_s.append(send(bt.at[2, core], bt.at[2, core], bsw, 3, sibling))
    for copy in b_s[1:]:
        copy.wait_recv()

    def coefs(to, carry):
        part = jnp.zeros((CB, 4 * cap), F32)
        for slot in range(4):
            for side in range(2):
                at = slot * v_dev + side * wide
                part = part + lax.dot_general(
                    bt[slot, side], pick[to, :, at : at + wide], NT, preferred_element_type=F32
                )
        bout[to] = part.astype(BF16)
        return carry

    lax.fori_loop(0, 4, coefs, 0)
    ahead, behind, across = lax.rem(y + 1, 4), lax.rem(y + 3, 4), lax.rem(y + 2, 4)
    h_f = [
        send(bout.at[across, low], bfr, hf, 0, up),
        send(bout.at[across, high], bfl, hf, 1, down),
    ]
    h_c = [
        send(bout.at[ahead], brec.at[y], hd, 0, up),
        send(bout.at[behind], brec.at[y], hd, 1, down),
    ]
    brec[y] = bout[y]

    h_f[0].wait_recv()
    h_c.append(send(bfr, brec.at[behind, low], hg, 0, up))
    h_f[1].wait_recv()
    h_c.append(send(bfl, brec.at[ahead, high], hg, 1, down))
    for copy in h_c:
        copy.wait_recv()
    for to in range(4):
        for i in range(4):
            part = brec[i, :, to * cap : (to + 1) * cap].astype(F32)
            part = jnp.concatenate([part, part]).T.astype(BF16)
            bsel[to, i * cap : (i + 1) * cap, :] = part
    gram(0)
    pass_on(3)
    for copy in s_c + a_c:
        copy.wait_recv()
    auxs[...] = auxb[0] + auxb[1] + auxb[2] + auxb[3]
    quarter_v = pl.ds(pl.multiple_of(x * own, own), own)
    dos_var = auxs[0:1, quarter_v]
    rss = auxs[0:1, v_dev:]
    whole = ssend[x].astype(F32)
    for d in range(3):
        whole = whole + srecv[d].astype(F32)
    whole = (whole / jnp.sqrt(dos_var)).T / jnp.sqrt(rss / freedom + 1e-05)
    zbuf[quarter_v, :] = whole.astype(BF16)
    z_c = [send(zbuf.at[quarter_v], zbuf.at[quarter_v], zg, d - 1, at_x(d)) for d in (1, 2, 3)]
    gram(1)
    gram(2)
    for copy in z_c:
        copy.wait_recv()
    z_out[...] = zbuf[...]
    g_c = gram(3)
    whole = gacc[x]
    for copy in g_c:
        copy.wait_recv()
    for d in range(3):
        whole = whole + grecv[d].astype(F32)
    g_out[...] = whole
    for copy in sent:
        copy.wait_send()


def shards(n_z, dosages, proteins, covariates, hit_index, hit_count):
    n_sample = lax.axis_size("sample")
    n_variant = lax.axis_size("variant")
    rows, v_dev = dosages.shape
    n_prot = proteins.shape[1]
    n_cov = covariates.shape[0]
    samples = rows * n_sample
    n_dest, p_own, slots = hit_index.shape
    flat = p_own * slots
    block_hits = max(p_own * 16, 2 * slots)
    most = 3 * block_hits // n_variant
    other = -(-(block_hits - most) // (n_variant - 1))
    cap = -(-(most + 3 * other) // 16) * 16
    def vmem(shape, dtype=BF16):
        return pltpu.VMEM(shape, dtype)

    def pair(shape):
        return [pltpu.SemaphoreType.DMA(shape)] * 2

    crows = rows // CHUNKS
    own = v_dev // 4
    scratch = [
        vmem((3, rows, v_dev)),
        vmem((rows, v_dev)),
        vmem((4, 4 * cap, 4 * v_dev)),
        vmem((CHUNKS, 4, 4 * cap, crows)),
        vmem((CHUNKS, 4, 4 * cap, crows)),
        vmem((CHUNKS, 2 * cap, crows)),
        vmem((CHUNKS, 2 * cap, crows)),
        vmem((4, CP, v_dev // 2 + n_prot + 128), F32),
        vmem((4, 2, CB, v_dev // 2)),
        vmem((2 * CB, v_dev)),
        vmem((n_prot, rows)),
        vmem((4, n_prot, own)),
        vmem((3, n_prot, own)),
        vmem((4, 8, v_dev + n_prot), F32),
        vmem((8, v_dev + n_prot), F32),
        vmem((v_dev, n_prot)),
        vmem((4, p_own, slots, slots), F32),
        vmem((3, p_own, slots, slots)),
        vmem((3, p_own, slots, slots)),
        vmem((CP, rows), F32),
        vmem((rows, 2 * CB)),
        vmem((2 * CB, rows)),
        vmem((16, flat), F32),
        vmem((16, flat), F32),
        vmem((16, flat), F32),
        vmem((16, cap, 128)),
        vmem((16, cap, 128)),
        vmem((4, flat, 4 * cap)),
        vmem((4, CB, 4 * cap)),
        vmem((4, CB, 4 * cap)),
        vmem((CB // 2, 4 * cap)),
        vmem((CB // 2, 4 * cap)),
        vmem((4, 4 * cap, 2 * CB)),
        *pair((CHUNKS, 2)),
        *pair((CHUNKS, 2)),
        *pair((CHUNKS, 3)),
        *pair((2,)),
        *pair((2,)),
        *pair((4,)),
        *pair((3,)),
        *pair((3,)),
        *pair((3,)),
        *pair((3,)),
        *pair((3,)),
        *pair((CHUNKS, 2)),
        *pair((CHUNKS, 2)),
        *pair((CHUNKS, 2)),
        *pair((2,)),
        *pair((2,)),
        *pair((2,)),
    ]
    z, g = pl.pallas_call(
        functools.partial(kernel, n_z, n_cov, cap, float(samples - n_cov)),
        out_shape=(
            jax.ShapeDtypeStruct((v_dev, n_prot), BF16),
            jax.ShapeDtypeStruct((p_own, slots, slots), F32),
        ),
        in_specs=[pl.BlockSpec(memory_space=pltpu.VMEM)] * 5,
        out_specs=(pl.BlockSpec(memory_space=pltpu.VMEM),) * 2,
        scratch_shapes=scratch,
        compiler_params=pltpu.CompilerParams(
            collective_id=0, has_side_effects=True, vmem_limit_bytes=58 * 1024 * 1024
        ),
    )(dosages, proteins, covariates, hit_index, hit_count[:, :, None])
    return (z.astype(F32), g / F32(samples))


def solution(mesh):
    in_specs = (
        P("sample", "variant"),
        P("sample", "protein"),
        P(None, "sample"),
        P(None, "protein", None),
        P(None, "protein"),
    )
    out_specs = (P("variant", "protein"), P(("sample", "variant", "protein"), None, None))
    n_z = 4 * (mesh.shape["protein"] // 2)
    return jax.shard_map(
        functools.partial(shards, n_z),
        mesh=mesh,
        in_specs=in_specs,
        out_specs=out_specs,
        check_vma=False,
    )
```

```python
import functools

import jax
import jax.numpy as jnp
from jax import lax
from jax.experimental import pallas as pl
from jax.experimental.pallas import tpu as pltpu
from jax.sharding import PartitionSpec as P

BF16 = jnp.bfloat16
F32 = jnp.float32
MESH = pl.DeviceIdType.MESH
BEST = lax.Precision.HIGHEST
NT = (((1,), (1,)), ((), ()))
CHUNKS = 4
CP = 48
CB = 64


def kernel(n_z, n_cov, cap, freedom, dos, prot, cov, hidx, hcnt, z_out, g_out, *scratch):
    (
        dall, d2own, pick, out, rec, fr, fl, arb, bt, bc, prt, ssend, srecv, auxb, auxs, zbuf,
        gacc, gsend, grecv, cf, ct, c2, ranks, places, slot_pos, lows, highs, place,
        bout, brec, bfr, bfl, bsel, *sems,
    ) = scratch
    ag, fw, sw, bag, bfw, bsw, ar, sc, ax, zg, gr, yd, yf, yg, hd, hf, hg = zip(sems[0::2], sems[1::2])

    x = lax.axis_index("sample")
    v = lax.axis_index("variant")
    q = lax.axis_index("protein")
    y, zl = lax.rem(v, 4), v // 4
    core, zh = lax.rem(q, 2), q // 2
    z = zh * 4 + zl

    def at_x(d):
        return (lax.rem(x + d, 4), v, q)

    def at_y(d):
        return (x, zl * 4 + lax.rem(y + d, 4), q)

    def at_z(d):
        there = lax.rem(z + d + n_z, n_z)
        return (x, lax.rem(there, 4) * 4 + y, (there // 4) * 2 + core)

    right, left, sibling = at_z(1), at_z(-1), (x, v, zh * 2 + 1 - core)
    up, down = at_y(1), at_y(3)

    neighbours = [at_x(1), at_x(2), at_x(3), up, down, right, left, sibling]
    barrier = pltpu.get_barrier_semaphore()
    for there in neighbours:
        pl.semaphore_signal(barrier, inc=1, device_id=there, device_id_type=MESH)
    pl.semaphore_wait(barrier, len(neighbours))

    sent = []

    def send(src, dst, sem, at, there):
        copy = pltpu.make_async_remote_copy(
            src_ref=src,
            dst_ref=dst,
            send_sem=sem[0].at[at],
            recv_sem=sem[1].at[at],
            device_id=there,
            device_id_type=MESH,
        )
        copy.start()
        sent.append(copy)
        return copy

    rows, v_dev = dos.shape
    n_prot = prot.shape[1]
    slots = hidx.shape[2]
    crows = rows // CHUNKS
    half = crows // 2
    quarter = half // 2
    wide = v_dev // 2
    mine = pl.multiple_of(core * half, half)
    copies = {}

    def piece(k, more=0, size=half):
        return pl.ds(pl.multiple_of(k * crows + core * half + more, quarter), size)

    def gather_own(k):
        part = dos.at[piece(k)]
        copies["a", k] = send(part, dall.at[0, piece(k)], ag, (k, 0), right)
        copies["b", k] = send(part, dall.at[2, piece(k)], ag, (k, 1), left)

    def gather_on(k):
        high, low = piece(k, quarter, quarter), piece(k, 0, quarter)
        copies["a", k].wait_recv()
        copies["c", k] = send(dall.at[0, high], dall.at[1, high], fw, (k, 0), right)
        copies["s0", k] = send(dall.at[0, piece(k)], dall.at[0, piece(k)], sw, (k, 0), sibling)
        copies["b", k].wait_recv()
        copies["d", k] = send(dall.at[2, low], dall.at[1, low], fw, (k, 1), left)
        copies["s2", k] = send(dall.at[2, piece(k)], dall.at[2, piece(k)], sw, (k, 2), sibling)

    def gather_far(k):
        copies["c", k].wait_recv()
        copies["d", k].wait_recv()
        copies["s1", k] = send(dall.at[1, piece(k)], dall.at[1, piece(k)], sw, (k, 1), sibling)

    def choose(k):
        here = pl.ds(k * crows, crows)
        for slot in range(3):
            copies["s%d" % slot, k].wait_recv()

        def one(d, carry):
            to = lax.rem(y + d, 4)
            part = lax.dot_general(
                pick[to, :, 0:v_dev], dos[here, :], NT, preferred_element_type=F32
            )
            for slot in range(3):
                part = part + lax.dot_general(
                    pick[to, :, (slot + 1) * v_dev : (slot + 2) * v_dev],
                    dall[slot, here, :],
                    NT,
                    preferred_element_type=F32,
                )
            out[k, to] = part.astype(BF16)
            return carry

        ahead, behind, across = lax.rem(y + 1, 4), lax.rem(y + 3, 4), lax.rem(y + 2, 4)
        first, second = pl.ds(0, 2 * cap), pl.ds(2 * cap, 2 * cap)
        one(2, 0)
        copies["f0", k] = send(out.at[k, across, first], fr.at[k], yf, (k, 0), up)
        copies["f1", k] = send(out.at[k, across, second], fl.at[k], yf, (k, 1), down)
        lax.fori_loop(3, 6, one, 0)
        copies["y0", k] = send(out.at[k, ahead], rec.at[k, y], yd, (k, 0), up)
        copies["y1", k] = send(out.at[k, behind], rec.at[k, y], yd, (k, 1), down)
        rec[k, y] = out[k, y]

    def pass_on(k):
        ahead, behind = lax.rem(y + 1, 4), lax.rem(y + 3, 4)
        first, second = pl.ds(0, 2 * cap), pl.ds(2 * cap, 2 * cap)
        copies["f0", k].wait_recv()
        copies["g0", k] = send(fr.at[k], rec.at[k, behind, first], yg, (k, 0), up)
        copies["f1", k].wait_recv()
        copies["g1", k] = send(fl.at[k], rec.at[k, ahead, second], yg, (k, 1), down)

    def gram(k):
        for name in ("y0", "y1", "g0", "g1"):
            copies[name, k].wait_recv()

        done = []
        for d in (2, 1, 3, 0):
            to = lax.rem(x + d, 4)
            lines = pl.ds(pl.multiple_of(to * cap, cap), cap)
            got = jnp.concatenate([rec[k, i, lines, :] for i in range(4)])
            fit = jnp.dot(
                bsel[to], c2[:, k * crows : (k + 1) * crows], preferred_element_type=F32
            )
            got = (got.astype(F32) - fit).astype(BF16)
            hits = jnp.dot(place[to], got, preferred_element_type=F32).astype(BF16)
            for p in range(4):
                h = hits[p * 128 : (p + 1) * 128]
                g = lax.dot_general(h, h, NT, preferred_element_type=F32)
                if k > 0:
                    g = gacc[to, p] + g
                if k == CHUNKS - 1 and d > 0:
                    gsend[d - 1, p] = g.astype(BF16)
                else:
                    gacc[to, p] = g
            if k == CHUNKS - 1 and d > 0:
                done.append(send(gsend.at[d - 1], grecv.at[d - 1], gr, d - 1, at_x(d)))
        return done

    gather_own(0)
    gather_own(1)

    flat = 4 * slots
    lane = lax.broadcasted_iota(jnp.int32, (1, slots), 1)
    lists, lives = [], []
    for yy in range(4):
        for s in range(4):
            g = s * 16 + zl * 4 + yy
            lists.append(jnp.concatenate([hidx[g, p : p + 1, :] for p in range(4)], axis=1))
            lives.append(
                jnp.concatenate([lane < hcnt[g, p : p + 1, :] for p in range(4)], axis=1)
            )
    lists = jnp.concatenate(lists).astype(F32)
    lives = jnp.concatenate([jnp.where(one, 1.0, 0.0) for one in lives])
    block = jnp.floor(lists * (1.0 / v_dev))
    far = jnp.floor(block * 0.25)
    line = block - 4.0 * far
    upper = jnp.where(
        lax.broadcasted_iota(jnp.int32, (flat, flat), 0)
        <= lax.broadcasted_iota(jnp.int32, (flat, flat), 1),
        1.0,
        0.0,
    ).astype(BF16)
    chosen = jnp.where(line == y.astype(F32), lives, 0.0)
    rank = jnp.dot(chosen.astype(BF16), upper, preferred_element_type=F32)
    ranks[...] = jnp.where(chosen > 0.0, rank, 0.0)
    slot = zl.astype(F32) - far
    slot = jnp.where(slot < 0.0, slot + 4.0, slot)
    places[...] = lists + (slot - block) * v_dev + 1.0
    pos_of = jnp.where(lives > 0.0, line * cap, -1.0)
    for i in range(4):
        member = jnp.where(line == i, lives, 0.0)
        rank = jnp.dot(member.astype(BF16), upper, preferred_element_type=F32)
        pos_of = pos_of + jnp.where(member > 0.0, rank - 1.0, 0.0)
    slot_pos[...] = pos_of

    def column(t, carry):
        order = lax.broadcasted_iota(jnp.int32, (cap, flat), 0).astype(F32) + 1.0
        found = jnp.where(ranks[pl.ds(t, 1), :] == order, places[pl.ds(t, 1), :], 0.0)
        found = jnp.sum(found, axis=1, keepdims=True) - 1.0
        high = jnp.floor(found * (1.0 / 256.0))
        lows[t] = jnp.broadcast_to(found - 256.0 * high, (cap, 128)).astype(BF16)
        highs[t] = jnp.broadcast_to(high, (cap, 128)).astype(BF16)
        return carry

    lax.fori_loop(0, 16, column, 0)

    near = lax.broadcasted_iota(jnp.int32, (cap, 128), 1).astype(F32)
    near = (near.astype(BF16), (near + 128.0).astype(BF16))
    one_b, zero_b = jnp.ones((cap, 128), BF16), jnp.zeros((cap, 128), BF16)

    def build(t, carry):
        lines = pl.ds(pl.multiple_of(lax.rem(t, 4) * cap, cap), cap)
        low_of, high_of = lows[t], highs[t]
        for part in range(4 * v_dev // 256):
            here = jnp.where(high_of == jnp.full((cap, 128), part, BF16), low_of, -one_b)
            for i in range(2):
                at = part * 256 + i * 128
                pick[t // 4, lines, at : at + 128] = jnp.where(here == near[i], one_b, zero_b)
        return carry

    lax.fori_loop(0, 16, build, 0)
    gather_on(0)
    gather_own(2)

    ours = pl.multiple_of(core * wide, wide)
    cf[0:n_cov, :] = cov[...]
    cf[n_cov:, :] = jnp.zeros((CP - n_cov, rows), F32)
    cv = cf[...]
    c_1 = cv.astype(BF16)
    c_2 = (cv - c_1.astype(F32)).astype(BF16)
    c_3 = (cv - c_1.astype(F32) - c_2.astype(F32)).astype(BF16)
    c3v = jnp.concatenate([c_1, c_2, c_3])
    gap = jnp.zeros((CB - CP, rows), F32)
    stacked = jnp.concatenate([c_1.astype(F32), gap, c_2.astype(F32), gap])
    c2[...] = stacked.astype(BF16)
    ct[...] = stacked.T.astype(BF16)
    cd = jnp.dot(c3v, dos[:, pl.ds(ours, wide)], preferred_element_type=F32)
    cq = jnp.dot(c3v, prot[...], preferred_element_type=F32)
    cc = lax.dot_general(cv, cv, NT, precision=BEST, preferred_element_type=F32)
    arb[x, :, 0:wide] = cd[0:CP] + cd[CP : 2 * CP] + cd[2 * CP :]
    arb[x, :, wide : wide + n_prot] = cq[0:CP] + cq[CP : 2 * CP] + cq[2 * CP :]
    arb[x, :, wide + n_prot :] = jnp.zeros((CP, 128), F32)
    arb[x, :, wide + n_prot : wide + n_prot + CP] = cc
    sums = [send(arb.at[x], arb.at[x], ar, d - 1, at_x(d)) for d in (1, 2, 3)]

    gather_on(1)
    gather_own(3)
    gather_far(0)
    choose(0)

    def put(s, carry):
        want = jnp.broadcast_to(slot_pos[pl.ds(y * 4 + s, 1), :], (128, flat)).T
        here = lax.broadcasted_iota(jnp.int32, (flat, 128), 1).astype(F32)
        for i in range(4 * cap // 128):
            place[s, :, i * 128 : (i + 1) * 128] = jnp.where(
                want == here + float(i * 128), 1.0, 0.0
            ).astype(BF16)
        return carry

    lax.fori_loop(0, 4, put, 0)

    gather_far(1)
    gather_on(2)
    choose(1)
    gather_on(3)
    pass_on(0)

    for copy in sums:
        copy.wait_recv()
    total = arb[0] + arb[1] + arb[2] + arb[3]
    lane = lax.broadcasted_iota(jnp.int32, (CP, 128), 1)
    row = lax.broadcasted_iota(jnp.int32, (CP, 128), 0)
    both = total[:, wide + n_prot :]
    both = both + jnp.where((lane == row) & (row >= n_cov), 1.0, 0.0)
    both = both + jnp.where(lane == row + 64, 1.0, 0.0)
    unit = lax.broadcasted_iota(jnp.int32, (CP, 1), 0)
    for i in range(n_cov):
        scaled = both[i : i + 1, :] / both[i : i + 1, i : i + 1]
        both = both - (both[:, i : i + 1] - jnp.where(unit == i, 1.0, 0.0)) * scaled
    inverse = pltpu.roll(both, 64, 1)[:, 0:CP]
    coef = jnp.dot(
        inverse, total[:, : wide + n_prot], precision=BEST, preferred_element_type=F32
    )

    bt[0, core, 0:CP, :] = coef[:, :wide].astype(BF16)
    bt[0, core, CP:CB, :] = jnp.zeros((CB - CP, wide), BF16)
    low, high = pl.ds(0, CB // 2), pl.ds(CB // 2, CB // 2)
    b_a = send(bt.at[0, core], bt.at[1, core], bag, 0, right)
    b_b = send(bt.at[0, core], bt.at[3, core], bag, 1, left)
    b_s = [send(bt.at[0, core], bt.at[0, core], bsw, 0, sibling)]

    gather_far(2)
    choose(2)
    b_a.wait_recv()
    b_c = send(bt.at[1, core, high], bt.at[2, core, high], bfw, 0, right)
    b_s.append(send(bt.at[1, core], bt.at[1, core], bsw, 1, sibling))
    b_b.wait_recv()
    b_d = send(bt.at[3, core, low], bt.at[2, core, low], bfw, 1, left)
    b_s.append(send(bt.at[3, core], bt.at[3, core], bsw, 2, sibling))

    b_s[0].wait_recv()
    gather_far(3)
    pass_on(1)

    cb = coef[:, wide:]
    ch = cb.astype(BF16)
    cm = (cb - ch.astype(F32)).astype(BF16)
    gap = jnp.zeros((CB - CP, n_prot), BF16)
    ctv = ct[...]
    fit = jnp.dot(ctv, jnp.concatenate([ch, gap, ch, gap]), preferred_element_type=F32)
    fit = fit + jnp.dot(ctv, jnp.concatenate([cm, gap, cm, gap]), preferred_element_type=F32)
    res = (prot[...].astype(F32) - fit).astype(BF16).astype(F32)
    auxb[x, :, v_dev:] = jnp.broadcast_to(
        jnp.sum(res * res, axis=0, keepdims=True), (8, n_prot)
    )
    prt[...] = res.T.astype(BF16)

    for side in range(2):
        part = bt[0, side]
        bc[0:CB, side * wide : (side + 1) * wide] = part
        bc[CB:, side * wide : (side + 1) * wide] = part


    def own_residual(k, squares):
        here = pl.ds(pl.multiple_of(k * crows, crows), crows)
        fit = jnp.dot(ct[here, :], bc[...], preferred_element_type=F32)
        res = dos[here, :].astype(F32) - fit
        d2own[here, :] = res.astype(BF16)
        return squares + jnp.sum(res * res, axis=0, keepdims=True)

    squares = lax.fori_loop(0, CHUNKS, own_residual, jnp.zeros((1, v_dev), F32))
    auxb[x, :, :v_dev] = jnp.broadcast_to(squares, (8, v_dev))
    own = v_dev // 4

    def score(i, carry):
        cols = pl.ds(pl.multiple_of(i * own, own), own)
        ssend[i] = jnp.dot(prt[...], d2own[:, cols], preferred_element_type=F32).astype(BF16)
        return carry

    lax.fori_loop(0, 4, score, 0)
    s_c = [
        send(ssend.at[lax.rem(x + d, 4)], srecv.at[d - 1], sc, d - 1, at_x(d)) for d in (1, 2, 3)
    ]
    a_c = [send(auxb.at[x], auxb.at[x], ax, d - 1, at_x(d)) for d in (1, 2, 3)]

    b_c.wait_recv()
    b_d.wait_recv()
    b_s.append(send(bt.at[2, core], bt.at[2, core], bsw, 3, sibling))
    for copy in b_s[1:]:
        copy.wait_recv()

    def coefs(to, carry):
        part = jnp.zeros((CB, 4 * cap), F32)
        for slot in range(4):
            for side in range(2):
                at = slot * v_dev + side * wide
                part = part + lax.dot_general(
                    bt[slot, side], pick[to, :, at : at + wide], NT, preferred_element_type=F32
                )
        bout[to] = part.astype(BF16)
        return carry

    lax.fori_loop(0, 4, coefs, 0)
    ahead, behind, across = lax.rem(y + 1, 4), lax.rem(y + 3, 4), lax.rem(y + 2, 4)
    h_f = [
        send(bout.at[across, low], bfr, hf, 0, up),
        send(bout.at[across, high], bfl, hf, 1, down),
    ]
    h_c = [
        send(bout.at[ahead], brec.at[y], hd, 0, up),
        send(bout.at[behind], brec.at[y], hd, 1, down),
    ]
    brec[y] = bout[y]

    choose(3)
    pass_on(2)
    h_f[0].wait_recv()
    h_c.append(send(bfr, brec.at[behind, low], hg, 0, up))
    h_f[1].wait_recv()
    h_c.append(send(bfl, brec.at[ahead, high], hg, 1, down))
    for copy in h_c:
        copy.wait_recv()
    for to in range(4):
        for i in range(4):
            part = brec[i, :, to * cap : (to + 1) * cap].astype(F32)
            part = jnp.concatenate([part, part]).T.astype(BF16)
            bsel[to, i * cap : (i + 1) * cap, :] = part
    gram(0)
    gram(1)
    pass_on(3)
    for copy in s_c + a_c:
        copy.wait_recv()
    auxs[...] = auxb[0] + auxb[1] + auxb[2] + auxb[3]
    quarter_v = pl.ds(pl.multiple_of(x * own, own), own)
    dos_var = auxs[0:1, quarter_v]
    rss = auxs[0:1, v_dev:]
    whole = ssend[x].astype(F32)
    for d in range(3):
        whole = whole + srecv[d].astype(F32)
    whole = (whole / jnp.sqrt(dos_var)).T / jnp.sqrt(rss / freedom + 1e-05)
    zbuf[quarter_v, :] = whole.astype(BF16)
    z_c = [send(zbuf.at[quarter_v], zbuf.at[quarter_v], zg, d - 1, at_x(d)) for d in (1, 2, 3)]
    gram(2)
    for copy in z_c:
        copy.wait_recv()
    z_out[...] = zbuf[...]
    g_c = gram(3)
    whole = gacc[x]
    for copy in g_c:
        copy.wait_recv()
    for d in range(3):
        whole = whole + grecv[d].astype(F32)
    g_out[...] = whole
    for copy in sent:
        copy.wait_send()


def shards(n_z, dosages, proteins, covariates, hit_index, hit_count):
    n_sample = lax.axis_size("sample")
    n_variant = lax.axis_size("variant")
    rows, v_dev = dosages.shape
    n_prot = proteins.shape[1]
    n_cov = covariates.shape[0]
    samples = rows * n_sample
    n_dest, p_own, slots = hit_index.shape
    flat = p_own * slots
    block_hits = max(p_own * 16, 2 * slots)
    most = 3 * block_hits // n_variant
    other = -(-(block_hits - most) // (n_variant - 1))
    cap = -(-(most + 3 * other) // 16) * 16
    def vmem(shape, dtype=BF16):
        return pltpu.VMEM(shape, dtype)

    def pair(shape):
        return [pltpu.SemaphoreType.DMA(shape)] * 2

    crows = rows // CHUNKS
    own = v_dev // 4
    scratch = [
        vmem((3, rows, v_dev)),
        vmem((rows, v_dev)),
        vmem((4, 4 * cap, 4 * v_dev)),
        vmem((CHUNKS, 4, 4 * cap, crows)),
        vmem((CHUNKS, 4, 4 * cap, crows)),
        vmem((CHUNKS, 2 * cap, crows)),
        vmem((CHUNKS, 2 * cap, crows)),
        vmem((4, CP, v_dev // 2 + n_prot + 128), F32),
        vmem((4, 2, CB, v_dev // 2)),
        vmem((2 * CB, v_dev)),
        vmem((n_prot, rows)),
        vmem((4, n_prot, own)),
        vmem((3, n_prot, own)),
        vmem((4, 8, v_dev + n_prot), F32),
        vmem((8, v_dev + n_prot), F32),
        vmem((v_dev, n_prot)),
        vmem((4, p_own, slots, slots), F32),
        vmem((3, p_own, slots, slots)),
        vmem((3, p_own, slots, slots)),
        vmem((CP, rows), F32),
        vmem((rows, 2 * CB)),
        vmem((2 * CB, rows)),
        vmem((16, flat), F32),
        vmem((16, flat), F32),
        vmem((16, flat), F32),
        vmem((16, cap, 128)),
        vmem((16, cap, 128)),
        vmem((4, flat, 4 * cap)),
        vmem((4, CB, 4 * cap)),
        vmem((4, CB, 4 * cap)),
        vmem((CB // 2, 4 * cap)),
        vmem((CB // 2, 4 * cap)),
        vmem((4, 4 * cap, 2 * CB)),
        *pair((CHUNKS, 2)),
        *pair((CHUNKS, 2)),
        *pair((CHUNKS, 3)),
        *pair((2,)),
        *pair((2,)),
        *pair((4,)),
        *pair((3,)),
        *pair((3,)),
        *pair((3,)),
        *pair((3,)),
        *pair((3,)),
        *pair((CHUNKS, 2)),
        *pair((CHUNKS, 2)),
        *pair((CHUNKS, 2)),
        *pair((2,)),
        *pair((2,)),
        *pair((2,)),
    ]
    z, g = pl.pallas_call(
        functools.partial(kernel, n_z, n_cov, cap, float(samples - n_cov)),
        out_shape=(
            jax.ShapeDtypeStruct((v_dev, n_prot), BF16),
            jax.ShapeDtypeStruct((p_own, slots, slots), F32),
        ),
        in_specs=[pl.BlockSpec(memory_space=pltpu.VMEM)] * 5,
        out_specs=(pl.BlockSpec(memory_space=pltpu.VMEM),) * 2,
        scratch_shapes=scratch,
        compiler_params=pltpu.CompilerParams(
            collective_id=0, has_side_effects=True, vmem_limit_bytes=58 * 1024 * 1024
        ),
    )(dosages, proteins, covariates, hit_index, hit_count[:, :, None])
    return (z.astype(F32), g / F32(samples))


def solution(mesh):
    in_specs = (
        P("sample", "variant"),
        P("sample", "protein"),
        P(None, "sample"),
        P(None, "protein", None),
        P(None, "protein"),
    )
    out_specs = (P("variant", "protein"), P(("sample", "variant", "protein"), None, None))
    n_z = 4 * (mesh.shape["protein"] // 2)
    return jax.shard_map(
        functools.partial(shards, n_z),
        mesh=mesh,
        in_specs=in_specs,
        out_specs=out_specs,
        check_vma=False,
    )
```

```python
import functools

import jax
import jax.numpy as jnp
from jax import lax
from jax.experimental import pallas as pl
from jax.experimental.pallas import tpu as pltpu
from jax.sharding import PartitionSpec as P

BF16 = jnp.bfloat16
F32 = jnp.float32
MESH = pl.DeviceIdType.MESH
BEST = lax.Precision.HIGHEST
NT = (((1,), (1,)), ((), ()))
CHUNKS = 4
CP = 48
CB = 64


def kernel(n_z, n_cov, cap, freedom, dos, prot, cov, hidx, hcnt, z_out, g_out, *scratch):
    (
        dall, d2own, pick, out, rec, arb, bt, bc, prt, ssend, srecv, auxb, auxs, zbuf,
        gacc, gsend, grecv, cf, ct, c2, ranks, places, slot_pos, lows, highs, place,
        bout, brec, bsel, *sems,
    ) = scratch
    ag, fw, sw, bag, bfw, bsw, ar, sc, ax, zg, gr, yd, hd = zip(sems[0::2], sems[1::2])

    x = lax.axis_index("sample")
    v = lax.axis_index("variant")
    q = lax.axis_index("protein")
    y, zl = lax.rem(v, 4), v // 4
    core, zh = lax.rem(q, 2), q // 2
    z = zh * 4 + zl

    def at_x(d):
        return (lax.rem(x + d, 4), v, q)

    def at_y(d):
        return (x, zl * 4 + lax.rem(y + d, 4), q)

    def at_z(d):
        there = lax.rem(z + d + n_z, n_z)
        return (x, lax.rem(there, 4) * 4 + y, (there // 4) * 2 + core)

    right, left, sibling = at_z(1), at_z(-1), (x, v, zh * 2 + 1 - core)
    up, down, opposite = at_y(1), at_y(3), at_y(2)

    neighbours = [at_x(1), at_x(2), at_x(3), up, down, opposite, right, left, sibling]
    barrier = pltpu.get_barrier_semaphore()
    for there in neighbours:
        pl.semaphore_signal(barrier, inc=1, device_id=there, device_id_type=MESH)
    pl.semaphore_wait(barrier, len(neighbours))

    sent = []

    def send(src, dst, sem, at, there):
        copy = pltpu.make_async_remote_copy(
            src_ref=src,
            dst_ref=dst,
            send_sem=sem[0].at[at],
            recv_sem=sem[1].at[at],
            device_id=there,
            device_id_type=MESH,
        )
        copy.start()
        sent.append(copy)
        return copy

    rows, v_dev = dos.shape
    n_prot = prot.shape[1]
    slots = hidx.shape[2]
    crows = rows // CHUNKS
    half = crows // 2
    quarter = half // 2
    wide = v_dev // 2
    mine = pl.multiple_of(core * half, half)
    copies = {}

    def piece(k, more=0, size=half):
        return pl.ds(pl.multiple_of(k * crows + core * half + more, quarter), size)

    def gather_own(k):
        part = dos.at[piece(k)]
        copies["a", k] = send(part, dall.at[0, piece(k)], ag, (k, 0), right)
        copies["b", k] = send(part, dall.at[2, piece(k)], ag, (k, 1), left)

    def gather_on(k):
        high, low = piece(k, quarter, quarter), piece(k, 0, quarter)
        copies["a", k].wait_recv()
        copies["c", k] = send(dall.at[0, high], dall.at[1, high], fw, (k, 0), right)
        copies["s0", k] = send(dall.at[0, piece(k)], dall.at[0, piece(k)], sw, (k, 0), sibling)
        copies["b", k].wait_recv()
        copies["d", k] = send(dall.at[2, low], dall.at[1, low], fw, (k, 1), left)
        copies["s2", k] = send(dall.at[2, piece(k)], dall.at[2, piece(k)], sw, (k, 2), sibling)

    def gather_far(k):
        copies["c", k].wait_recv()
        copies["d", k].wait_recv()
        copies["s1", k] = send(dall.at[1, piece(k)], dall.at[1, piece(k)], sw, (k, 1), sibling)

    def choose(k):
        here = pl.ds(k * crows, crows)
        for slot in range(3):
            copies["s%d" % slot, k].wait_recv()

        def one(d, carry):
            to = lax.rem(y + d, 4)
            part = lax.dot_general(
                pick[to, :, 0:v_dev], dos[here, :], NT, preferred_element_type=F32
            )
            for slot in range(3):
                part = part + lax.dot_general(
                    pick[to, :, (slot + 1) * v_dev : (slot + 2) * v_dev],
                    dall[slot, here, :],
                    NT,
                    preferred_element_type=F32,
                )
            out[k, to] = part.astype(BF16)
            return carry

        ahead, behind, across = lax.rem(y + 1, 4), lax.rem(y + 3, 4), lax.rem(y + 2, 4)
        one(2, 0)
        copies["y2", k] = send(out.at[k, across], rec.at[k, y], yd, (k, 2), opposite)
        lax.fori_loop(3, 6, one, 0)
        copies["y0", k] = send(out.at[k, ahead], rec.at[k, y], yd, (k, 0), up)
        copies["y1", k] = send(out.at[k, behind], rec.at[k, y], yd, (k, 1), down)
        rec[k, y] = out[k, y]

    def gram(k):
        for name in ("y0", "y1", "y2"):
            copies[name, k].wait_recv()

        done = []
        for d in (2, 1, 3, 0):
            to = lax.rem(x + d, 4)
            lines = pl.ds(pl.multiple_of(to * cap, cap), cap)
            got = jnp.concatenate([rec[k, i, lines, :] for i in range(4)])
            fit = jnp.dot(
                bsel[to], c2[:, k * crows : (k + 1) * crows], preferred_element_type=F32
            )
            got = (got.astype(F32) - fit).astype(BF16)
            hits = jnp.dot(place[to], got, preferred_element_type=F32).astype(BF16)
            for p in range(4):
                h = hits[p * 128 : (p + 1) * 128]
                g = lax.dot_general(h, h, NT, preferred_element_type=F32)
                if k > 0:
                    g = gacc[to, p] + g
                if k == CHUNKS - 1 and d > 0:
                    gsend[d - 1, p] = g.astype(BF16)
                else:
                    gacc[to, p] = g
            if k == CHUNKS - 1 and d > 0:
                done.append(send(gsend.at[d - 1], grecv.at[d - 1], gr, d - 1, at_x(d)))
        return done

    gather_own(0)
    gather_own(1)

    flat = 4 * slots
    lane = lax.broadcasted_iota(jnp.int32, (1, slots), 1)
    lists, lives = [], []
    for yy in range(4):
        for s in range(4):
            g = s * 16 + zl * 4 + yy
            lists.append(jnp.concatenate([hidx[g, p : p + 1, :] for p in range(4)], axis=1))
            lives.append(
                jnp.concatenate([lane < hcnt[g, p : p + 1, :] for p in range(4)], axis=1)
            )
    lists = jnp.concatenate(lists).astype(F32)
    lives = jnp.concatenate([jnp.where(one, 1.0, 0.0) for one in lives])
    block = jnp.floor(lists * (1.0 / v_dev))
    far = jnp.floor(block * 0.25)
    line = block - 4.0 * far
    upper = jnp.where(
        lax.broadcasted_iota(jnp.int32, (flat, flat), 0)
        <= lax.broadcasted_iota(jnp.int32, (flat, flat), 1),
        1.0,
        0.0,
    ).astype(BF16)
    chosen = jnp.where(line == y.astype(F32), lives, 0.0)
    rank = jnp.dot(chosen.astype(BF16), upper, preferred_element_type=F32)
    ranks[...] = jnp.where(chosen > 0.0, rank, 0.0)
    slot = zl.astype(F32) - far
    slot = jnp.where(slot < 0.0, slot + 4.0, slot)
    places[...] = lists + (slot - block) * v_dev + 1.0
    pos_of = jnp.where(lives > 0.0, line * cap, -1.0)
    for i in range(4):
        member = jnp.where(line == i, lives, 0.0)
        rank = jnp.dot(member.astype(BF16), upper, preferred_element_type=F32)
        pos_of = pos_of + jnp.where(member > 0.0, rank - 1.0, 0.0)
    slot_pos[...] = pos_of

    def column(t, carry):
        order = lax.broadcasted_iota(jnp.int32, (cap, flat), 0).astype(F32) + 1.0
        found = jnp.where(ranks[pl.ds(t, 1), :] == order, places[pl.ds(t, 1), :], 0.0)
        found = jnp.sum(found, axis=1, keepdims=True) - 1.0
        high = jnp.floor(found * (1.0 / 256.0))
        lows[t] = jnp.broadcast_to(found - 256.0 * high, (cap, 128)).astype(BF16)
        highs[t] = jnp.broadcast_to(high, (cap, 128)).astype(BF16)
        return carry

    lax.fori_loop(0, 16, column, 0)

    near = lax.broadcasted_iota(jnp.int32, (cap, 128), 1).astype(F32)
    near = (near.astype(BF16), (near + 128.0).astype(BF16))
    one_b, zero_b = jnp.ones((cap, 128), BF16), jnp.zeros((cap, 128), BF16)

    def build(t, carry):
        lines = pl.ds(pl.multiple_of(lax.rem(t, 4) * cap, cap), cap)
        low_of, high_of = lows[t], highs[t]
        for part in range(4 * v_dev // 256):
            here = jnp.where(high_of == jnp.full((cap, 128), part, BF16), low_of, -one_b)
            for i in range(2):
                at = part * 256 + i * 128
                pick[t // 4, lines, at : at + 128] = jnp.where(here == near[i], one_b, zero_b)
        return carry

    lax.fori_loop(0, 16, build, 0)
    gather_on(0)
    gather_own(2)

    ours = pl.multiple_of(core * wide, wide)
    cf[0:n_cov, :] = cov[...]
    cf[n_cov:, :] = jnp.zeros((CP - n_cov, rows), F32)
    cv = cf[...]
    c_1 = cv.astype(BF16)
    c_2 = (cv - c_1.astype(F32)).astype(BF16)
    c_3 = (cv - c_1.astype(F32) - c_2.astype(F32)).astype(BF16)
    c3v = jnp.concatenate([c_1, c_2, c_3])
    gap = jnp.zeros((CB - CP, rows), F32)
    stacked = jnp.concatenate([c_1.astype(F32), gap, c_2.astype(F32), gap])
    c2[...] = stacked.astype(BF16)
    ct[...] = stacked.T.astype(BF16)
    cd = jnp.dot(c3v, dos[:, pl.ds(ours, wide)], preferred_element_type=F32)
    cq = jnp.dot(c3v, prot[...], preferred_element_type=F32)
    cc = lax.dot_general(cv, cv, NT, precision=BEST, preferred_element_type=F32)
    arb[x, :, 0:wide] = cd[0:CP] + cd[CP : 2 * CP] + cd[2 * CP :]
    arb[x, :, wide : wide + n_prot] = cq[0:CP] + cq[CP : 2 * CP] + cq[2 * CP :]
    arb[x, :, wide + n_prot :] = jnp.zeros((CP, 128), F32)
    arb[x, :, wide + n_prot : wide + n_prot + CP] = cc
    sums = [send(arb.at[x], arb.at[x], ar, d - 1, at_x(d)) for d in (1, 2, 3)]

    gather_on(1)
    gather_own(3)
    gather_far(0)
    choose(0)

    def put(s, carry):
        want = jnp.broadcast_to(slot_pos[pl.ds(y * 4 + s, 1), :], (128, flat)).T
        here = lax.broadcasted_iota(jnp.int32, (flat, 128), 1).astype(F32)
        for i in range(4 * cap // 128):
            place[s, :, i * 128 : (i + 1) * 128] = jnp.where(
                want == here + float(i * 128), 1.0, 0.0
            ).astype(BF16)
        return carry

    lax.fori_loop(0, 4, put, 0)

    gather_far(1)
    gather_on(2)
    choose(1)
    gather_on(3)

    for copy in sums:
        copy.wait_recv()
    total = arb[0] + arb[1] + arb[2] + arb[3]
    lane = lax.broadcasted_iota(jnp.int32, (CP, 128), 1)
    row = lax.broadcasted_iota(jnp.int32, (CP, 128), 0)
    both = total[:, wide + n_prot :]
    both = both + jnp.where((lane == row) & (row >= n_cov), 1.0, 0.0)
    both = both + jnp.where(lane == row + 64, 1.0, 0.0)
    unit = lax.broadcasted_iota(jnp.int32, (CP, 1), 0)
    for i in range(n_cov):
        scaled = both[i : i + 1, :] / both[i : i + 1, i : i + 1]
        both = both - (both[:, i : i + 1] - jnp.where(unit == i, 1.0, 0.0)) * scaled
    inverse = pltpu.roll(both, 64, 1)[:, 0:CP]
    coef = jnp.dot(
        inverse, total[:, : wide + n_prot], precision=BEST, preferred_element_type=F32
    )

    bt[0, core, 0:CP, :] = coef[:, :wide].astype(BF16)
    bt[0, core, CP:CB, :] = jnp.zeros((CB - CP, wide), BF16)
    low, high = pl.ds(0, CB // 2), pl.ds(CB // 2, CB // 2)
    b_a = send(bt.at[0, core], bt.at[1, core], bag, 0, right)
    b_b = send(bt.at[0, core], bt.at[3, core], bag, 1, left)
    b_s = [send(bt.at[0, core], bt.at[0, core], bsw, 0, sibling)]

    gather_far(2)
    choose(2)
    b_a.wait_recv()
    b_c = send(bt.at[1, core, high], bt.at[2, core, high], bfw, 0, right)
    b_s.append(send(bt.at[1, core], bt.at[1, core], bsw, 1, sibling))
    b_b.wait_recv()
    b_d = send(bt.at[3, core, low], bt.at[2, core, low], bfw, 1, left)
    b_s.append(send(bt.at[3, core], bt.at[3, core], bsw, 2, sibling))

    b_s[0].wait_recv()
    gather_far(3)

    cb = coef[:, wide:]
    ch = cb.astype(BF16)
    cm = (cb - ch.astype(F32)).astype(BF16)
    gap = jnp.zeros((CB - CP, n_prot), BF16)
    ctv = ct[...]
    fit = jnp.dot(ctv, jnp.concatenate([ch, gap, ch, gap]), preferred_element_type=F32)
    fit = fit + jnp.dot(ctv, jnp.concatenate([cm, gap, cm, gap]), preferred_element_type=F32)
    res = (prot[...].astype(F32) - fit).astype(BF16).astype(F32)
    auxb[x, :, v_dev:] = jnp.broadcast_to(
        jnp.sum(res * res, axis=0, keepdims=True), (8, n_prot)
    )
    prt[...] = res.T.astype(BF16)

    for side in range(2):
        part = bt[0, side]
        bc[0:CB, side * wide : (side + 1) * wide] = part
        bc[CB:, side * wide : (side + 1) * wide] = part


    def own_residual(k, squares):
        here = pl.ds(pl.multiple_of(k * crows, crows), crows)
        fit = jnp.dot(ct[here, :], bc[...], preferred_element_type=F32)
        res = dos[here, :].astype(F32) - fit
        d2own[here, :] = res.astype(BF16)
        return squares + jnp.sum(res * res, axis=0, keepdims=True)

    squares = lax.fori_loop(0, CHUNKS, own_residual, jnp.zeros((1, v_dev), F32))
    auxb[x, :, :v_dev] = jnp.broadcast_to(squares, (8, v_dev))
    own = v_dev // 4

    def score(i, carry):
        cols = pl.ds(pl.multiple_of(i * own, own), own)
        ssend[i] = jnp.dot(prt[...], d2own[:, cols], preferred_element_type=F32).astype(BF16)
        return carry

    lax.fori_loop(0, 4, score, 0)
    s_c = [
        send(ssend.at[lax.rem(x + d, 4)], srecv.at[d - 1], sc, d - 1, at_x(d)) for d in (1, 2, 3)
    ]
    a_c = [send(auxb.at[x], auxb.at[x], ax, d - 1, at_x(d)) for d in (1, 2, 3)]

    b_c.wait_recv()
    b_d.wait_recv()
    b_s.append(send(bt.at[2, core], bt.at[2, core], bsw, 3, sibling))
    for copy in b_s[1:]:
        copy.wait_recv()

    def coefs(to, carry):
        part = jnp.zeros((CB, 4 * cap), F32)
        for slot in range(4):
            for side in range(2):
                at = slot * v_dev + side * wide
                part = part + lax.dot_general(
                    bt[slot, side], pick[to, :, at : at + wide], NT, preferred_element_type=F32
                )
        bout[to] = part.astype(BF16)
        return carry

    lax.fori_loop(0, 4, coefs, 0)
    ahead, behind, across = lax.rem(y + 1, 4), lax.rem(y + 3, 4), lax.rem(y + 2, 4)
    h_c = [
        send(bout.at[across], brec.at[y], hd, 2, opposite),
        send(bout.at[ahead], brec.at[y], hd, 0, up),
        send(bout.at[behind], brec.at[y], hd, 1, down),
    ]
    brec[y] = bout[y]

    choose(3)

    for copy in s_c + a_c:
        copy.wait_recv()
    auxs[...] = auxb[0] + auxb[1] + auxb[2] + auxb[3]
    quarter_v = pl.ds(pl.multiple_of(x * own, own), own)
    dos_var = auxs[0:1, quarter_v]
    rss = auxs[0:1, v_dev:]
    whole = ssend[x].astype(F32)
    for d in range(3):
        whole = whole + srecv[d].astype(F32)
    whole = (whole / jnp.sqrt(dos_var)).T / jnp.sqrt(rss / freedom + 1e-05)
    zbuf[quarter_v, :] = whole.astype(BF16)
    z_c = [send(zbuf.at[quarter_v], zbuf.at[quarter_v], zg, d - 1, at_x(d)) for d in (1, 2, 3)]

    for copy in h_c:
        copy.wait_recv()
    for to in range(4):
        for i in range(4):
            part = brec[i, :, to * cap : (to + 1) * cap].astype(F32)
            part = jnp.concatenate([part, part]).T.astype(BF16)
            bsel[to, i * cap : (i + 1) * cap, :] = part
    gram(0)
    gram(1)
    gram(2)
    g_c = gram(3)
    for copy in z_c:
        copy.wait_recv()
    z_out[...] = zbuf[...]
    whole = gacc[x]
    for copy in g_c:
        copy.wait_recv()
    for d in range(3):
        whole = whole + grecv[d].astype(F32)
    g_out[...] = whole
    for copy in sent:
        copy.wait_send()


def shards(n_z, dosages, proteins, covariates, hit_index, hit_count):
    n_sample = lax.axis_size("sample")
    n_variant = lax.axis_size("variant")
    rows, v_dev = dosages.shape
    n_prot = proteins.shape[1]
    n_cov = covariates.shape[0]
    samples = rows * n_sample
    n_dest, p_own, slots = hit_index.shape
    flat = p_own * slots
    block_hits = max(p_own * 16, 2 * slots)
    most = 3 * block_hits // n_variant
    other = -(-(block_hits - most) // (n_variant - 1))
    cap = -(-(most + 3 * other) // 16) * 16
    def vmem(shape, dtype=BF16):
        return pltpu.VMEM(shape, dtype)

    def pair(shape):
        return [pltpu.SemaphoreType.DMA(shape)] * 2

    crows = rows // CHUNKS
    own = v_dev // 4
    scratch = [
        vmem((3, rows, v_dev)),
        vmem((rows, v_dev)),
        vmem((4, 4 * cap, 4 * v_dev)),
        vmem((CHUNKS, 4, 4 * cap, crows)),
        vmem((CHUNKS, 4, 4 * cap, crows)),
        vmem((4, CP, v_dev // 2 + n_prot + 128), F32),
        vmem((4, 2, CB, v_dev // 2)),
        vmem((2 * CB, v_dev)),
        vmem((n_prot, rows)),
        vmem((4, n_prot, own)),
        vmem((3, n_prot, own)),
        vmem((4, 8, v_dev + n_prot), F32),
        vmem((8, v_dev + n_prot), F32),
        vmem((v_dev, n_prot)),
        vmem((4, p_own, slots, slots), F32),
        vmem((3, p_own, slots, slots)),
        vmem((3, p_own, slots, slots)),
        vmem((CP, rows), F32),
        vmem((rows, 2 * CB)),
        vmem((2 * CB, rows)),
        vmem((16, flat), F32),
        vmem((16, flat), F32),
        vmem((16, flat), F32),
        vmem((16, cap, 128)),
        vmem((16, cap, 128)),
        vmem((4, flat, 4 * cap)),
        vmem((4, CB, 4 * cap)),
        vmem((4, CB, 4 * cap)),
        vmem((4, 4 * cap, 2 * CB)),
        *pair((CHUNKS, 2)),
        *pair((CHUNKS, 2)),
        *pair((CHUNKS, 3)),
        *pair((2,)),
        *pair((2,)),
        *pair((4,)),
        *pair((3,)),
        *pair((3,)),
        *pair((3,)),
        *pair((3,)),
        *pair((3,)),
        *pair((CHUNKS, 3)),
        *pair((3,)),
    ]
    z, g = pl.pallas_call(
        functools.partial(kernel, n_z, n_cov, cap, float(samples - n_cov)),
        out_shape=(
            jax.ShapeDtypeStruct((v_dev, n_prot), BF16),
            jax.ShapeDtypeStruct((p_own, slots, slots), F32),
        ),
        in_specs=[pl.BlockSpec(memory_space=pltpu.VMEM)] * 5,
        out_specs=(pl.BlockSpec(memory_space=pltpu.VMEM),) * 2,
        scratch_shapes=scratch,
        compiler_params=pltpu.CompilerParams(
            collective_id=0, has_side_effects=True, vmem_limit_bytes=58 * 1024 * 1024
        ),
    )(dosages, proteins, covariates, hit_index, hit_count[:, :, None])
    return (z.astype(F32), g / F32(samples))


def solution(mesh):
    in_specs = (
        P("sample", "variant"),
        P("sample", "protein"),
        P(None, "sample"),
        P(None, "protein", None),
        P(None, "protein"),
    )
    out_specs = (P("variant", "protein"), P(("sample", "variant", "protein"), None, None))
    n_z = 4 * (mesh.shape["protein"] // 2)
    return jax.shard_map(
        functools.partial(shards, n_z),
        mesh=mesh,
        in_specs=in_specs,
        out_specs=out_specs,
        check_vma=False,
    )
```
